128 devices in a mesh: dp: 8 (over x, core), seq: 16 (over y, z).
Axes of the slice: x: 4, y: 4, z: 4, core: 2. Of those that a mesh axis runs over, the one named last changes fastest.
Arguments:
- hidden: bfloat16 [16384, 8192], P(('dp', 'seq')), may hold values from -24 to 24
- queries: bfloat16 [16384, 4096], P(('dp', 'seq')), may hold values from -120 to 120
- kv_weight: bfloat16 [8192, 1024], replicated, may hold values from -0.0625 to 0.0625
- value_projection_bias: float32 [512], replicated, may hold values from -4 to 4
- cotangent: bfloat16 [16384, 4096], P(('dp', 'seq')), may hold values from -6 to 6
- lengths: int32 [8, 8], P('dp'), may hold values from 1 to 1024, 2048 in all within a row
Outputs:
- attended: bfloat16 [16384, 4096], P(('dp', 'seq'))
- query_grad: bfloat16 [16384, 4096], P(('dp', 'seq'))
- hidden_grad: bfloat16 [16384, 8192], P(('dp', 'seq'))
- weight_grad: float32 [8192, 1024], P(('dp', 'seq'))
The draws below stay inside these ranges and needn't reach their ends.
Inputs may be any that keep to these rules, and one draw needn't show every extreme that they name: The lengths of a row sum to 2048; in every row the longest document has exactly 1024 tokens.
All inputs are finite; a program needn't handle non-finite values.
Results may differ from the reference program's by a relative error of at most 0.025.
Values may be sent and summed in bfloat16 or wider, within the bound.
A program may use at most 192 MiB of HBM per device.

```python
import math
import jax
import jax.numpy as jnp
import numpy as np
from jax import lax

D = 8192
QUERY_HEADS = 32
KEY_VALUE_HEADS = 4
HEAD_SIZE = 128
DOCS = 8
TOK_DEV = 128
ROW_LEN = 2048
ROWS = 8
TOKENS = 16384
KVW = 1024
N_DP = 8
N_SEQ = 16


def draw_queries(key, part):
    key = jax.random.fold_in(key, 11)
    values = jax.random.normal(key, (TOKENS, QUERY_HEADS * HEAD_SIZE), jnp.float32)
    return jnp.clip(values, -6.0, 6.0).astype(jnp.bfloat16)


def raised(values, own_key, source, target, blocks, factor):
    def block_of(dim):
        return (jnp.arange(values.shape[dim]) // (values.shape[dim] // blocks)).reshape((-1,) + (1,) * (values.ndim - 1 - dim))

    first = jax.random.permutation(own_key, blocks)[block_of(target)]
    far = (block_of(target) + blocks // 2) % blocks
    return jnp.where((block_of(source) == first) | (block_of(source) == far), factor * values, values)


def steps_of(key, shape, shards, smallest, high):
    def one(axis_at, blocks):
        draws = jax.random.uniform(jax.random.fold_in(jax.random.fold_in(key, 6), axis_at), (blocks,), jnp.float32, smallest / len(shards), high / len(shards))
        return jnp.repeat(jnp.exp(draws), shape[axis_at] // blocks).reshape((-1,) + (1,) * (len(shape) - axis_at - 1))

    factor_of = one(*shards[0])
    for cut in shards[1:]:
        factor_of = factor_of * one(*cut)
    return factor_of


def split_up(count, total, limit, slope):
    weights = [(1 << 20) // math.isqrt(grade ** slope) + 1 for grade in range(2, count + 1)]
    surplus, holding = total - limit - (count - 1), [1] * (count - 1)
    while surplus > 0:
        candidates = [i for i in range(count - 1) if holding[i] < limit]
        mass, remaining = sum([weights[i] for i in candidates]), surplus
        for i in candidates:
            extra = min(limit - holding[i], max(1, remaining * weights[i] // mass), surplus)
            holding[i] = holding[i] + extra
            surplus = surplus - extra
    return np.array([limit] + holding)


def uneven(rng, count, total, most, lean):
    if count == 2:
        one = jax.random.randint(rng, (), max(1, total - most), min(most, total - 1) + 1)
        return jnp.stack([one, total - one])
    sizes = jnp.asarray(split_up(count, total, most, lean), jnp.int32)
    twos = (count - 1) // 2
    source_of, sink = sizes[1:1 + 2 * twos:2], sizes[2:2 + 2 * twos:2]
    margin = jnp.minimum(source_of - 1, most - sink)
    moved = jax.random.randint(jax.random.fold_in(rng, 1), (twos,), 0, 1 << 20) % (margin + 1)
    sizes = sizes.at[1:1 + 2 * twos:2].set(source_of - moved).at[2:2 + 2 * twos:2].set(sink + moved)
    return sizes[jax.random.permutation(jax.random.fold_in(rng, 2), count)]


def bell_draw(rng, dims, deviation, limit, shards=(), kind=jnp.bfloat16):
    loudness = steps_of(rng, dims, shards, -0.22, 0.18) if shards else 1.0
    array = jax.random.normal(rng, dims, jnp.float32) * deviation * loudness
    return jnp.minimum(jnp.maximum(array, -limit), limit).astype(kind)


def gaussian_with(rng, extent, scale, most, pieces, heavy, kind=jnp.bfloat16):
    result = scale * jax.random.normal(rng, extent, jnp.float32)
    if pieces:
        result = result * steps_of(rng, extent, pieces, -0.22, 0.18)
    return jnp.clip(raised(result, jax.random.fold_in(rng, 3), *heavy), -most, most).astype(kind)


def setup_inputs(seed: int = 0) -> dict:
    key_list = jax.random.split(jax.random.key(seed), 7)
    hidden = gaussian_with(key_list[0], (TOKENS, D), 1.0, 24.0, ((0, 128),), (0, 1, 128, 5.5))
    queries = draw_queries(jax.random.fold_in(key_list[6], 71), 0)
    kv_weight = bell_draw(key_list[2], (D, KVW), D ** -0.5, 0.0625)
    value_projection_bias = bell_draw(key_list[3], (KEY_VALUE_HEADS * HEAD_SIZE,), 1.0, 4.0, (), jnp.float32)
    cotangent = bell_draw(key_list[4], (TOKENS, QUERY_HEADS * HEAD_SIZE), 1.0, 6.0, ((0, 128),))
    lengths = jax.vmap(lambda own: uneven(own, DOCS, ROW_LEN, ROW_LEN // 2, 2))(jax.random.split(key_list[5], ROWS)).reshape((ROWS, DOCS)).astype(jnp.int32)
    return {"hidden": hidden, "queries": queries, "kv_weight": kv_weight, "value_projection_bias": value_projection_bias, "cotangent": cotangent, "lengths": lengths}


def attend(query_heads, key_value_pair, grad_heads, doc_ids):
    row_width_total = query_heads.shape[0]
    block_rows = min(512, row_width_total)
    block_count = row_width_total // block_rows
    score_scale = 1.0 / math.sqrt(HEAD_SIZE)
    key_part = key_value_pair[:, :HEAD_SIZE].astype(jnp.float32)
    value_part = key_value_pair[:, HEAD_SIZE:].astype(jnp.float32)
    position = jnp.arange(row_width_total, dtype=jnp.int32)

    def block_step(running, sliced):
        query_block, grad_block, doc_block, pos_block = sliced
        query_wide = query_block.astype(jnp.float32)
        grad_wide = grad_block.astype(jnp.float32)
        scores = jnp.einsum('qhd,kd->hqk', query_wide, key_part) * score_scale
        allowed = (doc_block[:, None] == doc_ids[None, :]) & (position[None, :] <= pos_block[:, None])
        scores = jnp.where(allowed[None], scores, -1e+30)
        row_max = lax.optimization_barrier(jnp.max(scores, axis=-1, keepdims=True))
        weights_raw = jnp.where(allowed[None], jnp.exp(scores - row_max), 0.0)
        probability = weights_raw / lax.optimization_barrier(jnp.sum(weights_raw, axis=-1, keepdims=True))
        prob_half = lax.optimization_barrier(probability.astype(jnp.bfloat16)).astype(jnp.float32)
        out_block = lax.optimization_barrier(jnp.einsum('hqk,kd->qhd', prob_half, value_part).astype(jnp.bfloat16))
        row_delta = lax.optimization_barrier(jnp.sum(grad_wide * out_block.astype(jnp.float32), axis=-1))
        prob_grad = jnp.einsum('qhd,kd->hqk', grad_wide, value_part)
        score_grad = (probability * (prob_grad - row_delta.T[:, :, None]) * score_scale).astype(jnp.bfloat16)
        score_wide = lax.optimization_barrier(score_grad).astype(jnp.float32)
        query_grad = jnp.einsum('hqk,kd->qhd', score_wide, key_part).astype(jnp.bfloat16)
        key_grad = running[0] + jnp.einsum('hqk,qhd->kd', score_wide, query_wide)
        value_grad = running[1] + jnp.einsum('hqk,qhd->kd', prob_half, grad_wide)
        return ((key_grad, value_grad), (out_block, query_grad))
    head_count = query_heads.shape[1]
    sliced = (query_heads.reshape(block_count, block_rows, head_count, HEAD_SIZE), grad_heads.reshape(block_count, block_rows, head_count, HEAD_SIZE), doc_ids.reshape(block_count, block_rows), position.reshape(block_count, block_rows))
    zero_grads = (jnp.zeros((row_width_total, HEAD_SIZE), jnp.float32), jnp.zeros((row_width_total, HEAD_SIZE), jnp.float32))
    (key_grad, value_grad), (out_blocks, grad_blocks) = lax.scan(block_step, zero_grads, sliced)
    return (out_blocks.reshape(row_width_total, head_count, HEAD_SIZE), grad_blocks.reshape(row_width_total, head_count, HEAD_SIZE), jnp.concatenate([key_grad, value_grad], axis=1))

def reference(hidden, queries, kv_weight, value_projection_bias, cotangent, lengths):
    row_width_total = TOK_DEV * N_SEQ
    group_width = QUERY_HEADS // KEY_VALUE_HEADS
    key_value_columns = 2 * KEY_VALUE_HEADS * HEAD_SIZE
    complete_bias = jnp.stack([jnp.zeros((KEY_VALUE_HEADS, HEAD_SIZE), jnp.float32), value_projection_bias.reshape(KEY_VALUE_HEADS, HEAD_SIZE)], axis=1).reshape(key_value_columns)
    position = jnp.arange(row_width_total, dtype=jnp.int32)

    def one_row(weight_grad, sliced):
        hidden_row, single_query_row, gradient_row, doc_lengths = sliced
        key_value_pair = (jnp.dot(hidden_row, kv_weight, preferred_element_type=jnp.float32) + complete_bias).astype(jnp.bfloat16)
        key_value_pair = key_value_pair.reshape(row_width_total, KEY_VALUE_HEADS, 2 * HEAD_SIZE).transpose(1, 0, 2)
        doc_ends = jnp.cumsum(doc_lengths).astype(jnp.int32)
        doc_ids = lax.optimization_barrier(jnp.sum((position[:, None] >= doc_ends[None, :]).astype(jnp.int32), axis=1)).astype(jnp.int32)
        grouped_queries = single_query_row.reshape(row_width_total, KEY_VALUE_HEADS, group_width, HEAD_SIZE).transpose(1, 0, 2, 3)
        gradient_groups = gradient_row.reshape(row_width_total, KEY_VALUE_HEADS, group_width, HEAD_SIZE).transpose(1, 0, 2, 3)

        def per_group(items):
            return attend(items[0], items[1], items[2], doc_ids)
        out_heads, qgrad_heads, kv_grads = lax.map(per_group, (grouped_queries, key_value_pair, gradient_groups))
        attended = out_heads.transpose(1, 0, 2, 3).reshape(row_width_total, QUERY_HEADS * HEAD_SIZE)
        query_grad = qgrad_heads.transpose(1, 0, 2, 3).reshape(row_width_total, QUERY_HEADS * HEAD_SIZE)
        key_value_gradient = kv_grads.transpose(1, 0, 2).reshape(row_width_total, key_value_columns).astype(jnp.bfloat16)
        hidden_grad = jnp.dot(key_value_gradient, kv_weight.T, preferred_element_type=jnp.float32).astype(jnp.bfloat16)
        weight_grad = weight_grad + jnp.dot(hidden_row.T, key_value_gradient, preferred_element_type=jnp.float32)
        return (weight_grad, (attended, query_grad, hidden_grad))
    sliced = (hidden.reshape(N_DP, row_width_total, D), queries.reshape(N_DP, row_width_total, QUERY_HEADS * HEAD_SIZE), cotangent.reshape(N_DP, row_width_total, QUERY_HEADS * HEAD_SIZE), lengths)
    weight_grad, (attended, query_grad, hidden_grad) = lax.scan(one_row, jnp.zeros((D, key_value_columns), jnp.float32), sliced)
    weight_grad = weight_grad * (1.0 / math.sqrt(TOKENS))
    return (attended.reshape(TOKENS, QUERY_HEADS * HEAD_SIZE), query_grad.reshape(TOKENS, QUERY_HEADS * HEAD_SIZE), hidden_grad.reshape(TOKENS, D), weight_grad)
```

```python
import math

import jax
import jax.numpy as jnp
from jax import lax
from jax.sharding import PartitionSpec as P

QUERY_HEADS = 32
KEY_VALUE_HEADS = 4
HEAD_SIZE = 128


def attend(query_heads, key_value_pair, grad_heads, doc_ids):
    row_width_total = query_heads.shape[0]
    head_count = query_heads.shape[1]
    block_rows = min(512, row_width_total)
    block_count = row_width_total // block_rows
    score_scale = 1.0 / math.sqrt(HEAD_SIZE)
    key_part = key_value_pair[:, :HEAD_SIZE]
    value_part = key_value_pair[:, HEAD_SIZE:]
    position = jnp.arange(row_width_total, dtype=jnp.int32)

    def block_step(running, sliced):
        query_block, grad_block, doc_block, pos_block = sliced
        scores = (
            jnp.einsum("qhd,kd->hqk", query_block, key_part, preferred_element_type=jnp.float32)
            * score_scale
        )
        allowed = (doc_block[:, None] == doc_ids[None, :]) & (
            position[None, :] <= pos_block[:, None]
        )
        scores = jnp.where(allowed[None], scores, -1e30)
        row_max = jnp.max(scores, axis=-1, keepdims=True)
        weights_raw = jnp.where(allowed[None], jnp.exp(scores - row_max), 0.0)
        probability = weights_raw / jnp.sum(weights_raw, axis=-1, keepdims=True)
        prob_half = probability.astype(jnp.bfloat16)
        out_block = jnp.einsum(
            "hqk,kd->qhd", prob_half, value_part, preferred_element_type=jnp.float32
        ).astype(jnp.bfloat16)
        row_delta = jnp.sum(grad_block.astype(jnp.float32) * out_block.astype(jnp.float32), axis=-1)
        prob_grad = jnp.einsum(
            "qhd,kd->hqk", grad_block, value_part, preferred_element_type=jnp.float32
        )
        score_grad = (probability * (prob_grad - row_delta.T[:, :, None]) * score_scale).astype(
            jnp.bfloat16
        )
        query_grad = jnp.einsum(
            "hqk,kd->qhd", score_grad, key_part, preferred_element_type=jnp.float32
        ).astype(jnp.bfloat16)
        key_grad = running[0] + jnp.einsum(
            "hqk,qhd->kd", score_grad, query_block, preferred_element_type=jnp.float32
        )
        value_grad = running[1] + jnp.einsum(
            "hqk,qhd->kd", prob_half, grad_block, preferred_element_type=jnp.float32
        )
        return ((key_grad, value_grad), (out_block, query_grad))

    sliced = (
        query_heads.reshape(block_count, block_rows, head_count, HEAD_SIZE),
        grad_heads.reshape(block_count, block_rows, head_count, HEAD_SIZE),
        doc_ids.reshape(block_count, block_rows),
        position.reshape(block_count, block_rows),
    )
    zero_grads = (
        jnp.zeros((row_width_total, HEAD_SIZE), jnp.float32),
        jnp.zeros((row_width_total, HEAD_SIZE), jnp.float32),
    )
    (key_grad, value_grad), (out_blocks, grad_blocks) = lax.scan(block_step, zero_grads, sliced)
    return (
        out_blocks.reshape(row_width_total, head_count, HEAD_SIZE),
        grad_blocks.reshape(row_width_total, head_count, HEAD_SIZE),
        jnp.concatenate([key_grad, value_grad], axis=1),
    )


def local(hidden, queries, kv_weight, value_projection_bias, cotangent, lengths):
    token_count = hidden.shape[0]
    sequence_count = lax.axis_size("seq")
    data_count = lax.axis_size("dp")
    row_width_total = token_count * sequence_count
    key_value_columns = 2 * KEY_VALUE_HEADS * HEAD_SIZE
    repeat_count = sequence_count // KEY_VALUE_HEADS
    factor = 1.0 / math.sqrt(row_width_total * data_count)
    query_heads = queries.reshape(token_count, QUERY_HEADS, HEAD_SIZE)
    grad_heads = cotangent.reshape(token_count, QUERY_HEADS, HEAD_SIZE)
    query_local, grad_local = (
        lax.all_to_all(query_heads, "seq", split_axis=1, concat_axis=0, tiled=True),
        lax.all_to_all(grad_heads, "seq", split_axis=1, concat_axis=0, tiled=True),
    )
    complete_bias = jnp.stack(
        [
            jnp.zeros((KEY_VALUE_HEADS, HEAD_SIZE), jnp.float32),
            value_projection_bias.reshape(KEY_VALUE_HEADS, HEAD_SIZE),
        ],
        axis=1,
    ).reshape(key_value_columns)
    key_value_pair = (
        jnp.dot(hidden, kv_weight, preferred_element_type=jnp.float32) + complete_bias
    ).astype(jnp.bfloat16)
    expanded = jnp.broadcast_to(
        key_value_pair.reshape(token_count, KEY_VALUE_HEADS, 1, 2 * HEAD_SIZE),
        (token_count, KEY_VALUE_HEADS, repeat_count, 2 * HEAD_SIZE),
    )
    expanded = expanded.reshape(token_count, sequence_count, 2 * HEAD_SIZE)
    kv_local = lax.all_to_all(expanded, "seq", split_axis=1, concat_axis=0, tiled=True).reshape(
        row_width_total, 2 * HEAD_SIZE
    )
    position = jnp.arange(row_width_total, dtype=jnp.int32)
    doc_ends = jnp.cumsum(lengths[0])
    doc_ids = jnp.sum((position[:, None] >= doc_ends[None, :]).astype(jnp.int32), axis=1)
    out_heads, qgrad_heads, kv_grad_local = attend(query_local, kv_local, grad_local, doc_ids)
    attended, query_grad = (
        lax.all_to_all(out_heads, "seq", split_axis=0, concat_axis=1, tiled=True),
        lax.all_to_all(qgrad_heads, "seq", split_axis=0, concat_axis=1, tiled=True),
    )
    key_value_pieces = lax.all_to_all(
        kv_grad_local.reshape(row_width_total, 1, 2 * HEAD_SIZE),
        "seq",
        split_axis=0,
        concat_axis=1,
        tiled=True,
    )
    key_value_gradient = jnp.sum(
        key_value_pieces.reshape(token_count, KEY_VALUE_HEADS, repeat_count, 2 * HEAD_SIZE), axis=2
    ).reshape(token_count, key_value_columns)
    key_value_gradient = key_value_gradient.astype(jnp.bfloat16)
    hidden_grad = jnp.einsum(
        "tc,dc->td", key_value_gradient, kv_weight, preferred_element_type=jnp.float32
    ).astype(jnp.bfloat16)
    hidden_columns = lax.all_to_all(
        hidden.reshape(token_count, data_count, -1), "dp", split_axis=1, concat_axis=0, tiled=True
    ).reshape(token_count * data_count, -1)
    gathered_gradient = lax.all_gather(key_value_gradient, "dp", axis=0, tiled=True)
    product = lax.dot_general(
        hidden_columns,
        gathered_gradient,
        (((0,), (0,)), ((), ())),
        preferred_element_type=jnp.float32,
    )
    weight_grad = lax.psum_scatter(product * factor, "seq", scatter_dimension=0, tiled=True)
    return (
        attended.reshape(token_count, QUERY_HEADS * HEAD_SIZE),
        query_grad.reshape(token_count, QUERY_HEADS * HEAD_SIZE),
        hidden_grad,
        weight_grad,
    )


def solution(mesh):
    in_specs = (
        P(("dp", "seq"), None),
        P(("dp", "seq"), None),
        P(),
        P(),
        P(("dp", "seq"), None),
        P("dp", None),
    )
    out_specs = (
        P(("dp", "seq"), None),
        P(("dp", "seq"), None),
        P(("dp", "seq"), None),
        P(("dp", "seq"), None),
    )
    return jax.shard_map(local, mesh=mesh, in_specs=in_specs, out_specs=out_specs, check_vma=False)
```

```python
import functools
import math

import jax
import jax.numpy as jnp
from jax import lax
from jax.experimental import pallas as pl
from jax.experimental.pallas import tpu as pltpu
from jax.sharding import PartitionSpec as P

GROUPS = 4
GROUP_HEADS = 8
HEAD = 128
PAIR = 2 * HEAD
TOK = 128
BACK = 8
SLOTS = BACK + 1
KEYS = SLOTS * TOK
D = 8192
N_DP = 8
N_SEQ = 16
D_PART = D // N_DP
D_OWN = D_PART // N_SEQ
SCALE = 1.0 / math.sqrt(HEAD)
LOG2E = 1.4426950408889634
FACTOR = 1.0 / math.sqrt(TOK * N_DP * N_SEQ)
F32 = jnp.float32
BF16 = jnp.bfloat16


def dot(a, b):
    return jnp.dot(a, b, preferred_element_type=F32)


def kernel(
    hidden_hbm, queries_hbm, weight_hbm, bias_ref, cot_hbm, lengths_ref,
    att_hbm, qgrad_hbm, hgrad_hbm, wgrad_hbm,
    hid, qry, cot, wgt, kv, mask, kt, vt, acc, att, qgr, hgr, wgr,
    dk_out, dk_in, dk_own, dkv, dkvt, hx, hxt, dall, w_out, w_in,
    in_sem, wgt_sem, kv_s, kv_r, dk_s, dk_r, hx_s, hx_r, ag_s, ag_r, rs_s, rs_r, out_sem,
):
    me = lax.axis_index("seq")
    row = lax.axis_index("dp")
    before = jnp.minimum(me, BACK)
    after = jnp.minimum(N_SEQ - 1 - me, BACK)

    in_hid = pltpu.make_async_copy(hidden_hbm, hid, in_sem.at[0])
    in_qry = pltpu.make_async_copy(queries_hbm, qry, in_sem.at[1])
    in_cot = pltpu.make_async_copy(cot_hbm, cot, in_sem.at[2])
    in_hid.start()

    def weight_copy(g):
        return pltpu.make_async_copy(
            weight_hbm.at[:, pl.ds(pl.multiple_of(g * PAIR, PAIR), PAIR)], wgt.at[g], wgt_sem.at[g]
        )

    def start_weight(g, _):
        weight_copy(g).start()
        return 0

    lax.fori_loop(0, GROUPS, start_weight, 0)
    in_qry.start()
    in_cot.start()

    barrier = pltpu.get_barrier_semaphore()

    def greet_seq(i, _):
        pl.semaphore_signal(
            barrier, inc=1, device_id={"seq": lax.rem(me + 1 + i, N_SEQ)},
            device_id_type=pl.DeviceIdType.MESH,
        )
        return 0

    def greet_dp(i, _):
        pl.semaphore_signal(
            barrier, inc=1, device_id={"dp": lax.rem(row + 1 + i, N_DP)},
            device_id_type=pl.DeviceIdType.MESH,
        )
        return 0

    lax.fori_loop(0, N_SEQ - 1, greet_seq, 0)
    lax.fori_loop(0, N_DP - 1, greet_dp, 0)

    p_pos = me * TOK + lax.broadcasted_iota(jnp.int32, (1, TOK), 1)
    start = jnp.zeros((1, TOK), jnp.int32)
    end = jnp.int32(0)
    for i in range(lengths_ref.shape[1]):
        end = end + lengths_ref[0, i]
        start = jnp.where(p_pos >= end, end, start)
    k_pos = (me - BACK) * TOK + lax.broadcasted_iota(jnp.int32, (KEYS, TOK), 0)
    mask[...] = jnp.where((k_pos >= start) & (k_pos <= p_pos), 0.0, -1e30).astype(F32)

    def clear(s, _):
        for g in range(GROUPS):
            kv[g, pl.ds(pl.multiple_of(s * TOK, TOK), TOK), :] = jnp.zeros((TOK, PAIR), BF16)
        return 0

    lax.fori_loop(0, BACK - before, clear, 0)

    in_hid.wait()
    pl.semaphore_wait(barrier, N_SEQ - 1 + N_DP - 1)

    def hx_copy(i):
        peer = lax.rem(row + 1 + i, N_DP)
        return pltpu.make_async_remote_copy(
            src_ref=hid.at[:, pl.ds(pl.multiple_of(peer * D_PART, D_PART), D_PART)],
            dst_ref=hx.at[pl.ds(pl.multiple_of(row * TOK, TOK), TOK), :],
            send_sem=hx_s.at[i],
            recv_sem=hx_r.at[row],
            device_id={"dp": peer},
            device_id_type=pl.DeviceIdType.MESH,
        )

    hx_own = pltpu.make_async_copy(
        hid.at[:, pl.ds(pl.multiple_of(row * D_PART, D_PART), D_PART)],
        hx.at[pl.ds(pl.multiple_of(row * TOK, TOK), TOK), :],
        in_sem.at[3],
    )

    def kv_copy(g, d):
        return pltpu.make_async_remote_copy(
            src_ref=kv.at[g, pl.ds(BACK * TOK, TOK), :],
            dst_ref=kv.at[g, pl.ds(pl.multiple_of((BACK - 1 - d) * TOK, TOK), TOK), :],
            send_sem=kv_s.at[g, d],
            recv_sem=kv_r.at[g, BACK - 1 - d],
            device_id={"seq": jnp.minimum(me + 1 + d, N_SEQ - 1)},
            device_id_type=pl.DeviceIdType.MESH,
        )

    def project(g, _):
        weight_copy(g).wait()

        def step(i, total):
            cols = pl.ds(pl.multiple_of(i * 1024, 1024), 1024)
            return total + dot(hid[:, cols], wgt[g, cols, :])

        total = lax.fori_loop(0, D // 1024, step, jnp.zeros((TOK, PAIR), F32))
        kv[g, BACK * TOK :, :HEAD] = total[:, :HEAD].astype(BF16)
        kv[g, BACK * TOK :, HEAD:] = (total[:, HEAD:] + bias_ref[g]).astype(BF16)

        def send(d, _):
            kv_copy(g, d).start()
            return 0

        lax.fori_loop(0, after, send, 0)
        return 0

    lax.fori_loop(0, GROUPS, project, 0)

    def start_hx(i, _):
        hx_copy(i).start()
        return 0

    lax.fori_loop(0, N_DP - 1, start_hx, 0)
    hx_own.start()
    in_qry.wait()
    in_cot.wait()

    def dk_copy(g, d):
        return pltpu.make_async_remote_copy(
            src_ref=dk_out.at[g, pl.ds(pl.multiple_of((BACK - 1 - d) * TOK, TOK), TOK), :],
            dst_ref=dk_in.at[g, d],
            send_sem=dk_s.at[g, d],
            recv_sem=dk_r.at[g, d],
            device_id={"seq": jnp.maximum(me - 1 - d, 0)},
            device_id_type=pl.DeviceIdType.MESH,
        )

    def att_copy(g):
        cols = pl.ds(pl.multiple_of(g * 1024, 1024), 1024)
        return pltpu.make_async_copy(att.at[:, cols], att_hbm.at[:, cols], out_sem.at[0, g])

    def qgr_copy(g):
        cols = pl.ds(pl.multiple_of(g * 1024, 1024), 1024)
        return pltpu.make_async_copy(qgr.at[:, cols], qgrad_hbm.at[:, cols], out_sem.at[1, g])

    def attention(g):
        def arrive(d, _):
            kv_copy(g, BACK - 1 - (BACK - 1 - d)).wait_recv()
            return 0

        lax.fori_loop(0, before, arrive, 0)
        kt[...] = kv[g, :, :HEAD].T
        vt[...] = kv[g, :, HEAD:].T
        acc[...] = jnp.zeros((KEYS, PAIR), F32)

        def heads(c, _):
            cols = pl.ds(pl.multiple_of(g * 1024 + c * PAIR, PAIR), PAIR)
            q2 = qry[:, cols]
            o2 = cot[:, cols]
            q_rows = jnp.concatenate([q2[:, :HEAD], q2[:, HEAD:]], axis=0)
            o_rows = jnp.concatenate([o2[:, :HEAD], o2[:, HEAD:]], axis=0)
            q_t = jnp.concatenate([q2[:, :HEAD].T, q2[:, HEAD:].T], axis=1)
            o_t = jnp.concatenate([o2[:, :HEAD].T, o2[:, HEAD:].T], axis=1)
            bias = mask[...]
            s = dot(kv[g, :, :HEAD], q_t) + jnp.concatenate([bias, bias], axis=1)
            top = jnp.max(s, axis=0, keepdims=True)
            e = jnp.exp2((s - top) * (SCALE * LOG2E))
            inv = 1.0 / jnp.sum(e, axis=0, keepdims=True)
            prob = e * inv
            half = prob.astype(BF16)
            out_t = dot(vt[...], half)
            out_b = out_t.astype(BF16)
            delta = jnp.sum(o_t.astype(F32) * out_b.astype(F32), axis=0, keepdims=True)
            dp = dot(kv[g, :, HEAD:], o_t)
            ds = (prob * (dp - delta)).astype(BF16)
            dq_t = dot(kt[...], ds) * SCALE
            acc[:, :HEAD] += dot(ds, q_rows)
            acc[:, HEAD:] += dot(half, o_rows)
            att[:, cols] = jnp.concatenate(
                [out_t[:, :HEAD].T, out_t[:, HEAD:].T], axis=1
            ).astype(BF16)
            qgr[:, cols] = jnp.concatenate([dq_t[:, :HEAD].T, dq_t[:, HEAD:].T], axis=1).astype(
                BF16
            )
            return 0

        lax.fori_loop(0, GROUP_HEADS // 2, heads, 0)
        dk_out[g, :, :HEAD] = (acc[: BACK * TOK, :HEAD] * SCALE).astype(BF16)
        dk_out[g, :, HEAD:] = acc[: BACK * TOK, HEAD:].astype(BF16)
        dk_own[g, :, :HEAD] = acc[BACK * TOK :, :HEAD] * SCALE
        dk_own[g, :, HEAD:] = acc[BACK * TOK :, HEAD:]

        def send(d, _):
            dk_copy(g, d).start()
            return 0

        lax.fori_loop(0, before, send, 0)
        att_copy(g).start()
        qgr_copy(g).start()

    def ag_copy(g, i):
        return pltpu.make_async_remote_copy(
            src_ref=dkv.at[g],
            dst_ref=dall.at[g, pl.ds(pl.multiple_of(row * TOK, TOK), TOK), :],
            send_sem=ag_s.at[g, i],
            recv_sem=ag_r.at[g, row],
            device_id={"dp": lax.rem(row + 1 + i, N_DP)},
            device_id_type=pl.DeviceIdType.MESH,
        )

    def home(g):
        def arrive(d, total):
            dk_copy(g, d).wait_recv()
            return total + dk_in[g, d].astype(F32)

        total = lax.fori_loop(0, after, arrive, dk_own[g])
        half = total.astype(BF16)
        dkv[g] = half
        dall[g, pl.ds(pl.multiple_of(row * TOK, TOK), TOK), :] = half
        dkvt[pl.ds(pl.multiple_of(g * PAIR, PAIR), PAIR), :] = half.T

        def send(i, _):
            ag_copy(g, i).start()
            return 0

        lax.fori_loop(0, N_DP - 1, send, 0)

    def hx_arrive():
        def arrive(i, _):
            peer = lax.rem(row + 1 + i, N_DP)
            pltpu.make_async_remote_copy(
                src_ref=hid.at[:, pl.ds(0, D_PART)],
                dst_ref=hx.at[pl.ds(pl.multiple_of(peer * TOK, TOK), TOK), :],
                send_sem=hx_s.at[i],
                recv_sem=hx_r.at[peer],
                device_id={"dp": peer},
                device_id_type=pl.DeviceIdType.MESH,
            ).wait_recv()
            return 0

        lax.fori_loop(0, N_DP - 1, arrive, 0)
        hx_own.wait()

        def turn(i, _):
            rows = pl.ds(pl.multiple_of(i * TOK, TOK), TOK)
            hxt[:, rows] = hx[rows, :].T
            return 0

        lax.fori_loop(0, N_DP, turn, 0)

    def rs_copy(g, i):
        peer = lax.rem(me + 1 + i, N_SEQ)
        return pltpu.make_async_remote_copy(
            src_ref=w_out.at[g, pl.ds(pl.multiple_of(peer * D_OWN, D_OWN), D_OWN), :],
            dst_ref=w_in.at[g, me],
            send_sem=rs_s.at[g, i],
            recv_sem=rs_r.at[g, me],
            device_id={"seq": peer},
            device_id_type=pl.DeviceIdType.MESH,
        )

    def product(g):
        def arrive(i, _):
            peer = lax.rem(row + 1 + i, N_DP)
            pltpu.make_async_remote_copy(
                src_ref=dkv.at[g],
                dst_ref=dall.at[g, pl.ds(pl.multiple_of(peer * TOK, TOK), TOK), :],
                send_sem=ag_s.at[g, i],
                recv_sem=ag_r.at[g, peer],
                device_id={"dp": peer},
                device_id_type=pl.DeviceIdType.MESH,
            ).wait_recv()
            return 0

        lax.fori_loop(0, N_DP - 1, arrive, 0)

        def tile(i, _):
            rows = pl.ds(pl.multiple_of(i * 256, 256), 256)
            w_out[g, rows, :] = dot(hxt[rows, :], dall[g]).astype(BF16)
            return 0

        lax.fori_loop(0, D_PART // 256, tile, 0)

        def send(i, _):
            rs_copy(g, i).start()
            return 0

        lax.fori_loop(0, N_SEQ - 1, send, 0)

    def finish(g):
        own = w_out[g, pl.ds(pl.multiple_of(me * D_OWN, D_OWN), D_OWN), :].astype(F32)

        def arrive(i, total):
            peer = lax.rem(me + 1 + i, N_SEQ)
            pltpu.make_async_remote_copy(
                src_ref=w_out.at[g, pl.ds(0, D_OWN), :],
                dst_ref=w_in.at[g, peer],
                send_sem=rs_s.at[g, i],
                recv_sem=rs_r.at[g, peer],
                device_id={"seq": peer},
                device_id_type=pl.DeviceIdType.MESH,
            ).wait_recv()
            return total + w_in[g, peer].astype(F32)

        total = lax.fori_loop(0, N_SEQ - 1, arrive, own)
        wgr[:, pl.ds(pl.multiple_of(g * PAIR, PAIR), PAIR)] = total * FACTOR

    HG = 512

    def hgr_copy(i):
        cols = pl.ds(pl.multiple_of(i * HG, HG), HG)
        return pltpu.make_async_copy(hgr.at[:, cols], hgrad_hbm.at[:, cols], out_sem.at[2, i])

    def hidden_gradient(i, _):
        cols = pl.ds(pl.multiple_of(i * HG, HG), HG)
        total = dot(wgt[0, cols, :], dkvt[:PAIR, :])
        for g in range(1, GROUPS):
            total = total + dot(wgt[g, cols, :], dkvt[g * PAIR : (g + 1) * PAIR, :])
        hgr[:, cols] = total.T.astype(BF16)
        hgr_copy(i).start()
        return 0

    def stage(t, _):
        @pl.when(t < GROUPS)
        def _():
            attention(t)

        @pl.when((t >= 1) & (t <= GROUPS))
        def _():
            home(t - 1)

        @pl.when(t == 1)
        def _():
            hx_arrive()

        @pl.when(t == GROUPS)
        def _():
            lax.fori_loop(0, D // HG // 2, hidden_gradient, 0)

        @pl.when(t >= 2)
        def _():
            product(t - 2)

        return 0

    lax.fori_loop(0, GROUPS + 2, stage, 0)
    lax.fori_loop(D // HG // 2, D // HG, hidden_gradient, 0)

    def last(g, _):
        finish(g)
        return 0

    lax.fori_loop(0, GROUPS, last, 0)
    wgr_copy = pltpu.make_async_copy(wgr, wgrad_hbm, in_sem.at[4])
    wgr_copy.start()

    def drain(g, _):
        def kv_end(d, _):
            kv_copy(g, d).wait_send()
            return 0

        def dk_end(d, _):
            dk_copy(g, d).wait_send()
            return 0

        def ag_end(i, _):
            ag_copy(g, i).wait_send()
            return 0

        def rs_end(i, _):
            rs_copy(g, i).wait_send()
            return 0

        lax.fori_loop(0, after, kv_end, 0)
        lax.fori_loop(0, before, dk_end, 0)
        lax.fori_loop(0, N_DP - 1, ag_end, 0)
        lax.fori_loop(0, N_SEQ - 1, rs_end, 0)
        att_copy(g).wait()
        qgr_copy(g).wait()
        return 0

    def hx_end(i, _):
        hx_copy(i).wait_send()
        return 0

    def hgr_end(i, _):
        hgr_copy(i).wait()
        return 0

    lax.fori_loop(0, GROUPS, drain, 0)
    lax.fori_loop(0, N_DP - 1, hx_end, 0)
    lax.fori_loop(0, D // HG, hgr_end, 0)
    wgr_copy.wait()


def local(hidden, queries, kv_weight, value_projection_bias, cotangent, lengths):
    any_spec = pl.BlockSpec(memory_space=pl.ANY)
    vmem = pltpu.VMEM
    dma = pltpu.SemaphoreType.DMA
    width = GROUPS * GROUP_HEADS * HEAD
    return pl.pallas_call(
        kernel,
        out_shape=(
            jax.ShapeDtypeStruct((TOK, width), BF16),
            jax.ShapeDtypeStruct((TOK, width), BF16),
            jax.ShapeDtypeStruct((TOK, D), BF16),
            jax.ShapeDtypeStruct((D_OWN, GROUPS * PAIR), F32),
        ),
        in_specs=[
            any_spec,
            any_spec,
            any_spec,
            pl.BlockSpec(memory_space=pltpu.VMEM),
            any_spec,
            pl.BlockSpec(memory_space=pltpu.SMEM),
        ],
        out_specs=(any_spec,) * 4,
        scratch_shapes=[
            vmem((TOK, D), BF16),
            vmem((TOK, width), BF16),
            vmem((TOK, width), BF16),
            vmem((GROUPS, D, PAIR), BF16),
            vmem((GROUPS, KEYS, PAIR), BF16),
            vmem((KEYS, TOK), F32),
            vmem((HEAD, KEYS), BF16),
            vmem((HEAD, KEYS), BF16),
            vmem((KEYS, PAIR), F32),
            vmem((TOK, width), BF16),
            vmem((TOK, width), BF16),
            vmem((TOK, D), BF16),
            vmem((D_OWN, GROUPS * PAIR), F32),
            vmem((GROUPS, BACK * TOK, PAIR), BF16),
            vmem((GROUPS, BACK, TOK, PAIR), BF16),
            vmem((GROUPS, TOK, PAIR), F32),
            vmem((GROUPS, TOK, PAIR), BF16),
            vmem((GROUPS * PAIR, TOK), BF16),
            vmem((N_DP * TOK, D_PART), BF16),
            vmem((D_PART, N_DP * TOK), BF16),
            vmem((GROUPS, N_DP * TOK, PAIR), BF16),
            vmem((GROUPS, D_PART, PAIR), BF16),
            vmem((GROUPS, N_SEQ, D_OWN, PAIR), BF16),
            dma((5,)),
            dma((GROUPS,)),
            dma((GROUPS, BACK)),
            dma((GROUPS, BACK)),
            dma((GROUPS, BACK)),
            dma((GROUPS, BACK)),
            dma((N_DP,)),
            dma((N_DP,)),
            dma((GROUPS, N_DP)),
            dma((GROUPS, N_DP)),
            dma((GROUPS, N_SEQ)),
            dma((GROUPS, N_SEQ)),
            dma((3, 16)),
        ],
        compiler_params=pltpu.CompilerParams(
            collective_id=0, has_side_effects=True, vmem_limit_bytes=60 * 1024 * 1024
        ),
        cost_estimate=pl.CostEstimate(
            flops=14_000_000_000, bytes_accessed=26_000_000, transcendentals=5_000_000
        ),
    )(
        hidden,
        queries,
        kv_weight,
        value_projection_bias.reshape(GROUPS, 1, HEAD),
        cotangent,
        lengths,
    )


def solution(mesh):
    both = P(("dp", "seq"), None)
    return jax.shard_map(
        local,
        mesh=mesh,
        in_specs=(both, both, P(), P(), both, P("dp", None)),
        out_specs=(both,) * 4,
        check_vma=False,
    )
```

```python
import functools
import math

import jax
import jax.numpy as jnp
from jax import lax
from jax.experimental import pallas as pl
from jax.experimental.pallas import tpu as pltpu
from jax.sharding import PartitionSpec as P

GROUPS = 4
GROUP_HEADS = 8
HEAD = 128
PAIR = 2 * HEAD
TOK = 128
BACK = 8
SLOTS = BACK + 1
KEYS = SLOTS * TOK
D = 8192
N_DP = 8
N_SEQ = 16
D_PART = D // N_DP
D_OWN = D_PART // N_SEQ
SIDE = 4
BLOCK = 3 * TOK
HG = 2048
SCALE = 1.0 / math.sqrt(HEAD)
LOG2E = 1.4426950408889634
FACTOR = 1.0 / math.sqrt(TOK * N_DP * N_SEQ)
F32 = jnp.float32
BF16 = jnp.bfloat16


def dot(a, b):
    return jnp.dot(a, b, preferred_element_type=F32)


def kernel(
    hidden_hbm, queries_hbm, weight_hbm, bias_ref, cot_hbm, lengths_ref,
    att_hbm, qgrad_hbm, hgrad_hbm, wgrad_hbm,
    hid, qry, cot, wgt, kv, mask, kt, vt, q_rows, o_rows, o_cols, delta, prob, dscore, att, qgr, hgr, hgr_sum, wgr,
    dk_out, dk_in, dk_sum, dk_row, dk_col, dk_own, dkvt, hx, hxt, dall,
    w_out, w_in,
    in_sem, wgt_sem, kv_s, kv_r, dk_s, dk_r, dc_s, dc_r, hx_s, hx_r, ag_s, ag_r,
    rs_s, rs_r, out_sem,
):
    me = lax.axis_index("seq")
    row = lax.axis_index("dp")
    y, z = me // SIDE, lax.rem(me, SIDE)

    def remote(src, dst, send, recv, **peer):
        return pltpu.make_async_remote_copy(
            src_ref=src, dst_ref=dst, send_sem=send, recv_sem=recv, device_id=peer,
            device_id_type=pl.DeviceIdType.MESH,
        )

    def part(index, size):
        return pl.ds(pl.multiple_of(index * size, size), size)

    def each(count, body):
        def step(i, _):
            body(i)
            return 0

        lax.fori_loop(0, count, step, 0)

    def other(mine, i, count):
        return lax.rem(mine + 1 + i, count)

    def go(copy, wait):
        if wait:
            copy.wait_send()
        else:
            copy.start()

    in_hid = pltpu.make_async_copy(hidden_hbm, hid, in_sem.at[0])
    in_qry = pltpu.make_async_copy(queries_hbm, qry, in_sem.at[1])
    in_cot = pltpu.make_async_copy(cot_hbm, cot, in_sem.at[2])
    in_hid.start()

    def weight_copy(g):
        return pltpu.make_async_copy(weight_hbm.at[:, part(g, PAIR)], wgt.at[g], wgt_sem.at[g])

    weight_copy(0).start()
    weight_copy(1).start()

    barrier = pltpu.get_barrier_semaphore()

    def greet(**peer):
        pl.semaphore_signal(
            barrier, inc=1, device_id=peer, device_id_type=pl.DeviceIdType.MESH
        )

    each(N_SEQ - 1, lambda i: greet(seq=other(me, i, N_SEQ)))
    each(N_DP - 1, lambda i: greet(dp=other(row, i, N_DP)))

    p_pos = me * TOK + lax.broadcasted_iota(jnp.int32, (1, TOK), 1)
    start = jnp.zeros((1, TOK), jnp.int32)
    end = jnp.int32(0)
    for i in range(lengths_ref.shape[1]):
        end = end + lengths_ref[0, i]
        start = jnp.where(p_pos >= end, end, start)
    k_pos = (me - BACK) * TOK + lax.broadcasted_iota(jnp.int32, (KEYS, TOK), 0)
    mask[...] = jnp.where((k_pos >= start) & (k_pos <= p_pos), 0.0, -1e30).astype(F32)

    def clear(s):
        for g in range(GROUPS):
            kv[g, part(s, TOK), :] = jnp.zeros((TOK, PAIR), BF16)

    each(jnp.maximum(BACK - me, 0), clear)

    in_hid.wait()
    pl.semaphore_wait(barrier, N_SEQ - 1 + N_DP - 1)

    def kv_send(g, message, src, dst, peer):
        return remote(
            kv.at[g, part(src, TOK), :], kv.at[g, part(dst, TOK), :],
            kv_s.at[g, message], kv_r.at[g, dst], seq=peer,
        )

    def along_z(g, i, first, slot, wait):
        to = other(z, i, SIDE)
        dst = jnp.clip(slot + z - to, 0, BACK - 1)
        go(kv_send(g, first + i, slot, dst, y * SIDE + to), wait)

    def kv_first(g, wait=False):
        for rows in (1, 2):
            @pl.when(y + rows < SIDE)
            def _():
                to = jnp.minimum(me + SIDE * rows, N_SEQ - 1)
                go(kv_send(g, rows - 1, BACK, BACK - SIDE * rows, to), wait)

        def own(i):
            @pl.when(other(z, i, SIDE) > z)
            def _():
                along_z(g, i, 2, BACK, wait)

        each(SIDE - 1, own)

    def kv_arrive(g, s):
        kv_send(g, 0, BACK, s, me).wait_recv()

    def kv_second(g, wait=False):
        @pl.when(y >= 1)
        def _():
            if not wait:
                kv_arrive(g, SIDE)
            each(SIDE - 1, lambda i: along_z(g, i, 5, SIDE, wait))

        @pl.when(y >= 2)
        def _():
            if not wait:
                kv_arrive(g, 0)

            def two_before(i):
                @pl.when(other(z, i, SIDE) < z)
                def _():
                    along_z(g, i, 8, 0, wait)

            each(SIDE - 1, two_before)

    def kv_rest(g):
        def arrive(s):
            @pl.when((lax.rem(s, SIDE) != 0) & (me + s >= BACK))
            def _():
                kv_arrive(g, s)

        each(BACK, arrive)

    def project(g):
        weight_copy(g).wait()

        @pl.when(g + 2 < GROUPS)
        def _():
            weight_copy(g + 2).start()

        def step(i, total):
            cols = part(i, 2048)
            return total + dot(hid[:, cols], wgt[g, cols, :])

        total = lax.fori_loop(0, D // 2048, step, jnp.zeros((TOK, PAIR), F32))
        kv[g, BACK * TOK :, :HEAD] = total[:, :HEAD].astype(BF16)
        kv[g, BACK * TOK :, HEAD:] = (total[:, HEAD:] + bias_ref[g]).astype(BF16)

    def hx_copy(i, slot, peer):
        return remote(
            hid.at[:, part(peer, D_PART)], hx.at[part(slot, TOK), :],
            hx_s.at[i], hx_r.at[slot], dp=peer,
        )

    hx_own = pltpu.make_async_copy(
        hid.at[:, part(row, D_PART)], hx.at[part(row, TOK), :], in_sem.at[3]
    )
    def prepare(t):
        project(t)

        kv_first(t)

        @pl.when(t == 0)
        def _():
            each(N_DP - 1, lambda i: hx_copy(i, row, other(row, i, N_DP)).start())
            hx_own.start()
            in_qry.start()
            in_cot.start()

        @pl.when(t >= 2)
        def _():
            kv_second(t - 2)

    each(GROUPS, prepare)
    kv_second(2)
    in_qry.wait()
    in_cot.wait()

    def hx_arrive():
        def arrive(i):
            peer = other(row, i, N_DP)
            hx_copy(i, peer, peer).wait_recv()

        each(N_DP - 1, arrive)
        hx_own.wait()

        def turn(i):
            hxt[:, part(i, TOK)] = hx[part(i, TOK), :].T

        each(N_DP, turn)

    def att_copy(g):
        cols = part(g, 1024)
        return pltpu.make_async_copy(att.at[:, cols], att_hbm.at[:, cols], out_sem.at[0, g])

    def qgr_copy(g):
        cols = part(g, 1024)
        return pltpu.make_async_copy(qgr.at[:, cols], qgrad_hbm.at[:, cols], out_sem.at[1, g])

    WIDE = GROUP_HEADS * HEAD

    def stacked(wide):
        return jnp.concatenate([wide[:, h * HEAD : (h + 1) * HEAD] for h in range(GROUP_HEADS)], 0)

    def turned(wide):
        return jnp.concatenate([wide[:, h * HEAD : (h + 1) * HEAD].T for h in range(GROUP_HEADS)], 1)

    def forward(g):
        kt[...] = kv[g, :, :HEAD].T
        vt[...] = kv[g, :, HEAD:].T
        cols = part(g, WIDE)
        q_wide = qry[:, cols]
        o_wide = cot[:, cols]
        q_rows[...] = stacked(q_wide)
        o_rows[...] = stacked(o_wide)
        turned_o = turned(o_wide)
        o_cols[...] = turned_o
        s = dot(kv[g, :, :HEAD], turned(q_wide)) + jnp.concatenate([mask[...]] * GROUP_HEADS, 1)
        top = jnp.max(s, axis=0, keepdims=True)
        e = jnp.exp2((s - top) * (SCALE * LOG2E))
        inv = 1.0 / jnp.sum(e, axis=0, keepdims=True)
        half = (e * inv).astype(BF16)
        prob[...] = half
        out = dot(vt[...], half)
        out_b = out.astype(BF16).astype(F32)
        delta[...] = jnp.sum(turned_o.astype(F32) * out_b, axis=0, keepdims=True)
        att[:, cols] = turned(out).astype(BF16)
        att_copy(g).start()

    def backward(g, b):
        rows = part(b, BLOCK)
        half = prob[rows, :]
        dp = dot(kv[g, rows, HEAD:], o_cols[...])
        ds = (half.astype(F32) * (dp - delta[...])).astype(BF16)
        dscore[rows, :] = ds
        dk = dot(ds, q_rows[...]) * SCALE
        dv = dot(half, o_rows[...])
        dk_out[g, rows, :HEAD] = dk.astype(BF16)
        dk_out[g, rows, HEAD:] = dv.astype(BF16)
        dk_own[g, :, :HEAD] = dk[BLOCK - TOK :]
        dk_own[g, :, HEAD:] = dv[BLOCK - TOK :]
        each(BLOCK // TOK, lambda i: dk_send(g, b * (BLOCK // TOK) + i))

    def query_gradient(g):
        qgr[:, part(g, WIDE)] = turned(dot(kt[...], dscore[...]) * SCALE).astype(BF16)
        qgr_copy(g).start()

    def dk_copy(g, w, a, to):
        return remote(
            dk_out.at[g, part(w + SIDE * a, TOK), :], dk_in.at[g, w - 1, a],
            dk_s.at[g, w - 1, a], dk_r.at[g, w - 1, a], seq=to,
        )

    def dk_send(g, slot, wait=False):
        w, a = lax.rem(slot, SIDE), slot // SIDE

        @pl.when((w != 0) & (slot < BACK) & (me + slot >= BACK))
        def _():
            go(dk_copy(g, jnp.maximum(w, 1), a, y * SIDE + lax.rem(z + w, SIDE)), wait)

    def dc_copy(g, rows):
        return remote(
            dk_row.at[g, rows - 1], dk_col.at[g, rows - 1],
            dc_s.at[g, rows - 1], dc_r.at[g, rows - 1],
            seq=jnp.maximum(me - SIDE * rows, 0),
        )

    def dc_send(g, wait=False):
        for rows in (1, 2):
            @pl.when(y >= rows)
            def _():
                go(dc_copy(g, rows), wait)

    def row_sum(g):
        dk_sum[0] = dk_own[g]
        dk_sum[1] = dk_out[g, SIDE * TOK : (SIDE + 1) * TOK, :].astype(F32)
        dk_sum[2] = dk_out[g, :TOK, :].astype(F32)
        for w in range(1, SIDE):
            source = y * SIDE + lax.rem(z + SIDE - w, SIDE)
            nearer = jnp.where(z < w, 0, 1)
            for a in range(2):
                @pl.when(source + w + SIDE * a >= BACK)
                def _():
                    dk_copy(g, w, a, me).wait_recv()
                    at = nearer + 1 - a
                    dk_sum[at] = dk_sum[at] + dk_in[g, w - 1, a].astype(F32)

        dk_own[g] = dk_sum[0]
        dk_row[g, 0] = dk_sum[1].astype(BF16)
        dk_row[g, 1] = dk_sum[2].astype(BF16)
        dc_send(g)

    partner = row + 1 - 2 * lax.rem(row, 2)

    def ag_copy(g, message, slot, peer):
        block = dall.at[g, part(slot, TOK), :]
        return remote(block, block, ag_s.at[g, message], ag_r.at[g, slot], dp=peer)

    def along_x(i):
        return lax.rem(row + 2 + 2 * i, N_DP)

    def ag_send(g, wait=False):
        each(SIDE - 1, lambda i: go(ag_copy(g, i, row, along_x(i)), wait))
        go(ag_copy(g, SIDE - 1, row, partner), wait)

    def ag_relay(g, wait=False):
        def one(i):
            copy = ag_copy(g, SIDE + i, along_x(i), partner)
            if not wait:
                copy.wait_recv()
            go(copy, wait)

        each(SIDE - 1, one)

    def home(g):
        dk_sum[0] = dk_own[g]
        for rows in (1, 2):
            @pl.when(y + rows < SIDE)
            def _():
                dc_copy(g, rows).wait_recv()
                dk_sum[0] = dk_sum[0] + dk_col[g, rows - 1].astype(F32)

        half = dk_sum[0].astype(BF16)
        dall[g, part(row, TOK), :] = half
        ag_send(g)
        dkvt[part(g, PAIR), :] = half.T

    def rs_copy(g, i, slot, peer):
        return remote(
            w_out.at[g, part(peer, D_OWN), :], w_in.at[g, slot],
            rs_s.at[g, i], rs_r.at[g, slot], seq=peer,
        )

    def rs_send(g, wait=False):
        each(N_SEQ - 1, lambda i: go(rs_copy(g, i, me, other(me, i, N_SEQ)), wait))

    def product(g):
        ag_relay(g)
        each(SIDE, lambda i: ag_copy(g, 0, lax.rem(partner + 2 * i, N_DP), partner).wait_recv())

        w_out[g] = dot(hxt[...], dall[g]).astype(BF16)
        rs_send(g)

    def finish(g):
        def arrive(i, total):
            peer = other(me, i, N_SEQ)
            rs_copy(g, i, peer, peer).wait_recv()
            return total + w_in[g, peer].astype(F32)

        own = w_out[g, part(me, D_OWN), :].astype(F32)
        wgr[:, part(g, PAIR)] = lax.fori_loop(0, N_SEQ - 1, arrive, own) * FACTOR

    def hgr_copy(i):
        cols = part(i, HG)
        return pltpu.make_async_copy(hgr.at[:, cols], hgrad_hbm.at[:, cols], out_sem.at[2, i])

    def hidden_gradient(g, i):
        cols = part(i, HG)
        term = dot(wgt[g, cols, :], dkvt[part(g, PAIR), :])

        @pl.when(g == 0)
        def _():
            hgr_sum[cols, :] = term

        @pl.when((g > 0) & (g < GROUPS - 1))
        def _():
            hgr_sum[cols, :] += term

        @pl.when(g == GROUPS - 1)
        def _():
            hgr[:, cols] = (hgr_sum[cols, :] + term).T.astype(BF16)
            hgr_copy(i).start()

    def stage(g):
        kv_rest(g)
        forward(g)

        @pl.when(g == 0)
        def _():
            kv_second(3)

        @pl.when(g == 2)
        def _():
            hx_arrive()

        @pl.when(g >= 2)
        def _():
            row_sum(g - 2)

        each(KEYS // BLOCK, lambda b: backward(g, b))
        query_gradient(g)


    def hidden_part(g):
        each(D // HG, lambda i: hidden_gradient(g, i))

    each(GROUPS, stage)
    home(0)
    hidden_part(0)
    row_sum(2)
    home(1)
    hidden_part(1)
    product(0)
    row_sum(3)
    home(2)
    product(1)
    hidden_part(2)
    home(3)
    product(2)
    hidden_part(3)
    product(3)
    finish(0)
    finish(1)
    finish(2)
    finish(3)
    wgr_copy = pltpu.make_async_copy(wgr, wgrad_hbm, in_sem.at[4])
    wgr_copy.start()

    def drain(g):
        kv_first(g, True)
        kv_second(g, True)
        each(BACK, lambda i: dk_send(g, i, True))
        dc_send(g, True)
        ag_send(g, True)
        ag_relay(g, True)
        rs_send(g, True)
        att_copy(g).wait()
        qgr_copy(g).wait()

    each(GROUPS, drain)
    each(N_DP - 1, lambda i: hx_copy(i, row, other(row, i, N_DP)).wait_send())
    each(D // HG, lambda i: hgr_copy(i).wait())
    wgr_copy.wait()


def local(hidden, queries, kv_weight, value_projection_bias, cotangent, lengths):
    any_spec = pl.BlockSpec(memory_space=pl.ANY)
    vmem = pltpu.VMEM
    dma = pltpu.SemaphoreType.DMA
    width = GROUPS * GROUP_HEADS * HEAD
    return pl.pallas_call(
        kernel,
        out_shape=(
            jax.ShapeDtypeStruct((TOK, width), BF16),
            jax.ShapeDtypeStruct((TOK, width), BF16),
            jax.ShapeDtypeStruct((TOK, D), BF16),
            jax.ShapeDtypeStruct((D_OWN, GROUPS * PAIR), F32),
        ),
        in_specs=[
            any_spec,
            any_spec,
            any_spec,
            pl.BlockSpec(memory_space=pltpu.VMEM),
            any_spec,
            pl.BlockSpec(memory_space=pltpu.SMEM),
        ],
        out_specs=(any_spec,) * 4,
        scratch_shapes=[
            vmem((TOK, D), BF16),
            vmem((TOK, width), BF16),
            vmem((TOK, width), BF16),
            vmem((GROUPS, D, PAIR), BF16),
            vmem((GROUPS, KEYS, PAIR), BF16),
            vmem((KEYS, TOK), F32),
            vmem((HEAD, KEYS), BF16),
            vmem((HEAD, KEYS), BF16),
            vmem((GROUP_HEADS * HEAD, HEAD), BF16),
            vmem((GROUP_HEADS * HEAD, HEAD), BF16),
            vmem((HEAD, GROUP_HEADS * HEAD), BF16),
            vmem((1, GROUP_HEADS * HEAD), F32),
            vmem((KEYS, GROUP_HEADS * HEAD), BF16),
            vmem((KEYS, GROUP_HEADS * HEAD), BF16),
            vmem((TOK, width), BF16),
            vmem((TOK, width), BF16),
            vmem((TOK, D), BF16),
            vmem((D, TOK), F32),
            vmem((D_OWN, GROUPS * PAIR), F32),
            vmem((GROUPS, KEYS, PAIR), BF16),
            vmem((GROUPS, SIDE - 1, 2, TOK, PAIR), BF16),
            vmem((3, TOK, PAIR), F32),
            vmem((GROUPS, 2, TOK, PAIR), BF16),
            vmem((GROUPS, 2, TOK, PAIR), BF16),
            vmem((GROUPS, TOK, PAIR), F32),
            vmem((GROUPS * PAIR, TOK), BF16),
            vmem((N_DP * TOK, D_PART), BF16),
            vmem((D_PART, N_DP * TOK), BF16),
            vmem((GROUPS, N_DP * TOK, PAIR), BF16),
            vmem((GROUPS, D_PART, PAIR), BF16),
            vmem((GROUPS, N_SEQ, D_OWN, PAIR), BF16),
            dma((5,)),
            dma((GROUPS,)),
            dma((GROUPS, 11)),
            dma((GROUPS, BACK)),
            dma((GROUPS, SIDE - 1, 2)),
            dma((GROUPS, SIDE - 1, 2)),
            dma((GROUPS, 2)),
            dma((GROUPS, 2)),
            dma((N_DP,)),
            dma((N_DP,)),
            dma((GROUPS, N_DP)),
            dma((GROUPS, N_DP)),
            dma((GROUPS, N_SEQ)),
            dma((GROUPS, N_SEQ)),
            dma((3, 16)),
        ],
        compiler_params=pltpu.CompilerParams(
            collective_id=0, has_side_effects=True, vmem_limit_bytes=60 * 1024 * 1024
        ),
        cost_estimate=pl.CostEstimate(
            flops=14_000_000_000, bytes_accessed=26_000_000, transcendentals=5_000_000
        ),
    )(
        hidden,
        queries,
        kv_weight,
        value_projection_bias.reshape(GROUPS, 1, HEAD),
        cotangent,
        lengths,
    )


def solution(mesh):
    both = P(("dp", "seq"), None)
    return jax.shard_map(
        local,
        mesh=mesh,
        in_specs=(both, both, P(), P(), both, P("dp", None)),
        out_specs=(both,) * 4,
        check_vma=False,
    )
```

```python
import functools
import math

import jax
import jax.numpy as jnp
from jax import lax
from jax.experimental import pallas as pl
from jax.experimental.pallas import tpu as pltpu
from jax.sharding import PartitionSpec as P

GROUPS = 4
GROUP_HEADS = 8
HEAD = 128
PAIR = 2 * HEAD
TOK = 128
BACK = 8
SLOTS = BACK + 1
KEYS = SLOTS * TOK
D = 8192
N_DP = 8
N_SEQ = 16
D_PART = D // N_DP
D_OWN = D_PART // N_SEQ
SIDE = 4
BLOCK = 3 * TOK
HG = 4096
SCALE = 1.0 / math.sqrt(HEAD)
LOG2E = 1.4426950408889634
FACTOR = 1.0 / math.sqrt(TOK * N_DP * N_SEQ)
F32 = jnp.float32
BF16 = jnp.bfloat16


def dot(a, b):
    return jnp.dot(a, b, preferred_element_type=F32)


def kernel(
    hidden_hbm, queries_hbm, weight_hbm, bias_ref, cot_hbm, lengths_ref,
    att_hbm, qgrad_hbm, hgrad_hbm, wgrad_hbm,
    hid, qry, cot, wgt, kv, mask, kt, vt, q_rows, o_rows, o_cols, delta, prob, dscore, att, qgr, hgr, hgr_sum, wgr,
    dk_out, dk_in, dk_sum, dk_row, dk_col, dk_own, dkvt, hx, hxt, dall,
    w_out, w_in,
    in_sem, wgt_sem, kv_s, kv_r, dk_s, dk_r, dc_s, dc_r, hx_s, hx_r, ag_s, ag_r,
    rs_s, rs_r, out_sem,
):
    me = lax.axis_index("seq")
    row = lax.axis_index("dp")
    y, z = me // SIDE, lax.rem(me, SIDE)

    def remote(src, dst, send, recv, **peer):
        return pltpu.make_async_remote_copy(
            src_ref=src, dst_ref=dst, send_sem=send, recv_sem=recv, device_id=peer,
            device_id_type=pl.DeviceIdType.MESH,
        )

    def part(index, size):
        return pl.ds(pl.multiple_of(index * size, size), size)

    def each(count, body):
        def step(i, _):
            body(i)
            return 0

        lax.fori_loop(0, count, step, 0)

    def other(mine, i, count):
        return lax.rem(mine + 1 + i, count)

    def go(copy, wait):
        if wait:
            copy.wait_send()
        else:
            copy.start()

    in_hid = pltpu.make_async_copy(hidden_hbm, hid, in_sem.at[0])
    in_qry = pltpu.make_async_copy(queries_hbm, qry, in_sem.at[1])
    in_cot = pltpu.make_async_copy(cot_hbm, cot, in_sem.at[2])
    in_hid.start()

    def weight_copy(g):
        return pltpu.make_async_copy(weight_hbm.at[:, part(g, PAIR)], wgt.at[g], wgt_sem.at[g])

    weight_copy(0).start()
    weight_copy(1).start()

    barrier = pltpu.get_barrier_semaphore()

    def greet(**peer):
        pl.semaphore_signal(
            barrier, inc=1, device_id=peer, device_id_type=pl.DeviceIdType.MESH
        )

    each(N_SEQ - 1, lambda i: greet(seq=other(me, i, N_SEQ)))
    each(N_DP - 1, lambda i: greet(dp=other(row, i, N_DP)))

    p_pos = me * TOK + lax.broadcasted_iota(jnp.int32, (1, TOK), 1)
    start = jnp.zeros((1, TOK), jnp.int32)
    end = jnp.int32(0)
    for i in range(lengths_ref.shape[1]):
        end = end + lengths_ref[0, i]
        start = jnp.where(p_pos >= end, end, start)
    k_pos = (me - BACK) * TOK + lax.broadcasted_iota(jnp.int32, (KEYS, TOK), 0)
    mask[...] = jnp.where((k_pos >= start) & (k_pos <= p_pos), 0.0, -1e30).astype(F32)

    def clear(s):
        for g in range(GROUPS):
            kv[g, part(s, TOK), :] = jnp.zeros((TOK, PAIR), BF16)

    each(jnp.maximum(BACK - me, 0), clear)

    in_hid.wait()

    def project(g):
        weight_copy(g).wait()

        @pl.when(g + 2 < GROUPS)
        def _():
            weight_copy(g + 2).start()

        def step(i, total):
            cols = part(i, 4096)
            return total + dot(hid[:, cols], wgt[g, cols, :])

        total = lax.fori_loop(0, D // 4096, step, jnp.zeros((TOK, PAIR), F32))
        kv[g, BACK * TOK :, :HEAD] = total[:, :HEAD].astype(BF16)
        kv[g, BACK * TOK :, HEAD:] = (total[:, HEAD:] + bias_ref[g]).astype(BF16)

    project(0)
    pl.semaphore_wait(barrier, N_SEQ - 1 + N_DP - 1)

    def kv_send(g, message, src, dst, peer):
        return remote(
            kv.at[g, part(src, TOK), :], kv.at[g, part(dst, TOK), :],
            kv_s.at[g, message], kv_r.at[g, dst], seq=peer,
        )

    def along_z(g, i, first, slot, wait):
        to = other(z, i, SIDE)
        dst = jnp.clip(slot + z - to, 0, BACK - 1)
        go(kv_send(g, first + i, slot, dst, y * SIDE + to), wait)

    def kv_first(g, wait=False):
        for rows in (1, 2):
            @pl.when(y + rows < SIDE)
            def _():
                to = jnp.minimum(me + SIDE * rows, N_SEQ - 1)
                go(kv_send(g, rows - 1, BACK, BACK - SIDE * rows, to), wait)

    def sent(g, i):
        return (i != 1) | (g == 0)

    def kv_row(g, wait=False):
        def own(i):
            @pl.when((other(z, i, SIDE) > z) & sent(g, i))
            def _():
                along_z(g, i, 2, BACK, wait)

        each(SIDE - 1, own)

    def kv_arrive(g, s):
        kv_send(g, 0, BACK, s, me).wait_recv()

    def kv_second(g, wait=False):
        if not wait:
            @pl.when(g > 0)
            def _():
                kv_row(g)

        @pl.when(y >= 1)
        def _():
            if not wait:
                kv_arrive(g, SIDE)

            def row_before(i):
                @pl.when(sent(g, i))
                def _():
                    along_z(g, i, 5, SIDE, wait)

            each(SIDE - 1, row_before)

        @pl.when(y >= 2)
        def _():
            if not wait:
                kv_arrive(g, 0)

            def two_before(i):
                @pl.when((other(z, i, SIDE) < z) & sent(g, i))
                def _():
                    along_z(g, i, 8, 0, wait)

            each(SIDE - 1, two_before)

    up_from = jnp.where(z == SIDE - 1, 3, 7)
    down_from = jnp.where(z == 0, 5, 1)

    def kv_third(g, wait=False):
        for message, src, dst, to in (
            (11, up_from, 6, y * SIDE + lax.rem(z + 1, SIDE)),
            (12, down_from, 2, y * SIDE + lax.rem(z + SIDE - 1, SIDE)),
        ):
            @pl.when(me + src >= BACK)
            def _():
                if not wait:
                    kv_arrive(g, src)
                go(kv_send(g, message, src, dst, to), wait)

    def kv_rest(g):
        def arrive(s):
            passed = (g > 0) & ((s == up_from) | (s == down_from))

            @pl.when((lax.rem(s, SIDE) != 0) & (me + s >= BACK) & jnp.logical_not(passed))
            def _():
                kv_arrive(g, s)

        each(BACK, arrive)

    def hx_copy(i, slot, peer):
        return remote(
            hid.at[:, part(peer, D_PART)], hx.at[part(slot, TOK), :],
            hx_s.at[i], hx_r.at[slot], dp=peer,
        )

    hx_own = pltpu.make_async_copy(
        hid.at[:, part(row, D_PART)], hx.at[part(row, TOK), :], in_sem.at[3]
    )
    def prepare(t):
        @pl.when(t > 0)
        def _():
            project(t)

        kv_first(t)

        @pl.when(t == 0)
        def _():
            kv_row(t)

        @pl.when(t == 0)
        def _():
            each(N_DP - 1, lambda i: hx_copy(i, row, other(row, i, N_DP)).start())
            hx_own.start()
            in_qry.start()
            in_cot.start()

        @pl.when(t >= 2)
        def _():
            kv_second(t - 2)

    each(GROUPS, prepare)
    kv_second(2)
    in_qry.wait()
    in_cot.wait()

    def hx_arrive():
        def arrive(i):
            peer = other(row, i, N_DP)
            hx_copy(i, peer, peer).wait_recv()

        each(N_DP - 1, arrive)
        hx_own.wait()

        hxt[...] = hx[...].T

    def att_copy(g):
        cols = part(g, 1024)
        return pltpu.make_async_copy(att.at[:, cols], att_hbm.at[:, cols], out_sem.at[0, g])

    def qgr_copy(g):
        cols = part(g, 1024)
        return pltpu.make_async_copy(qgr.at[:, cols], qgrad_hbm.at[:, cols], out_sem.at[1, g])

    WIDE = GROUP_HEADS * HEAD

    def stacked(wide):
        return jnp.concatenate([wide[:, h * HEAD : (h + 1) * HEAD] for h in range(GROUP_HEADS)], 0)

    def turned(wide):
        return jnp.concatenate([wide[:, h * HEAD : (h + 1) * HEAD].T for h in range(GROUP_HEADS)], 1)

    def forward(g):
        kt[...] = kv[g, :, :HEAD].T
        vt[...] = kv[g, :, HEAD:].T
        cols = part(g, WIDE)
        q_wide = qry[:, cols]
        o_wide = cot[:, cols]
        q_rows[...] = stacked(q_wide)
        o_rows[...] = stacked(o_wide)
        turned_o = turned(o_wide)
        o_cols[...] = turned_o
        s = dot(kv[g, :, :HEAD], turned(q_wide)) + jnp.concatenate([mask[...]] * GROUP_HEADS, 1)
        top = jnp.max(s, axis=0, keepdims=True)
        e = jnp.exp2((s - top) * (SCALE * LOG2E))
        inv = 1.0 / jnp.sum(e, axis=0, keepdims=True)
        half = (e * inv).astype(BF16)
        prob[...] = half
        out = dot(vt[...], half)
        out_b = out.astype(BF16).astype(F32)
        delta[...] = jnp.sum(turned_o.astype(F32) * out_b, axis=0, keepdims=True)
        att[:, cols] = turned(out).astype(BF16)
        att_copy(g).start()

    def backward(g, b):
        rows = part(b, BLOCK)
        half = prob[rows, :]
        dp = dot(kv[g, rows, HEAD:], o_cols[...])
        ds = (half.astype(F32) * (dp - delta[...])).astype(BF16)
        dscore[rows, :] = ds
        dk = dot(ds, q_rows[...]) * SCALE
        dv = dot(half, o_rows[...])
        dk_out[g, rows, :HEAD] = dk.astype(BF16)
        dk_out[g, rows, HEAD:] = dv.astype(BF16)
        dk_own[g, :, :HEAD] = dk[BLOCK - TOK :]
        dk_own[g, :, HEAD:] = dv[BLOCK - TOK :]
        each(BLOCK // TOK, lambda i: dk_send(g, b * (BLOCK // TOK) + i))

    def query_gradient(g):
        qgr[:, part(g, WIDE)] = turned(dot(kt[...], dscore[...]) * SCALE).astype(BF16)
        qgr_copy(g).start()

    def dk_copy(g, w, a, to):
        return remote(
            dk_out.at[g, part(w + SIDE * a, TOK), :], dk_in.at[g, w - 1, a],
            dk_s.at[g, w - 1, a], dk_r.at[g, w - 1, a], seq=to,
        )

    def dk_send(g, slot, wait=False):
        w, a = lax.rem(slot, SIDE), slot // SIDE

        @pl.when((w != 0) & (slot < BACK) & (me + slot >= BACK))
        def _():
            go(dk_copy(g, jnp.maximum(w, 1), a, y * SIDE + lax.rem(z + w, SIDE)), wait)

    def dc_copy(g, rows):
        return remote(
            dk_row.at[g, rows - 1], dk_col.at[g, rows - 1],
            dc_s.at[g, rows - 1], dc_r.at[g, rows - 1],
            seq=jnp.maximum(me - SIDE * rows, 0),
        )

    def dc_send(g, wait=False):
        for rows in (1, 2):
            @pl.when(y >= rows)
            def _():
                go(dc_copy(g, rows), wait)

    def row_sum(g):
        dk_sum[0] = dk_own[g]
        dk_sum[1] = dk_out[g, SIDE * TOK : (SIDE + 1) * TOK, :].astype(F32)
        dk_sum[2] = dk_out[g, :TOK, :].astype(F32)
        for w in range(1, SIDE):
            source = y * SIDE + lax.rem(z + SIDE - w, SIDE)
            nearer = jnp.where(z < w, 0, 1)
            for a in range(2):
                @pl.when(source + w + SIDE * a >= BACK)
                def _():
                    dk_copy(g, w, a, me).wait_recv()
                    at = nearer + 1 - a
                    dk_sum[at] = dk_sum[at] + dk_in[g, w - 1, a].astype(F32)

        dk_own[g] = dk_sum[0]
        dk_row[g, 0] = dk_sum[1].astype(BF16)
        dk_row[g, 1] = dk_sum[2].astype(BF16)
        dc_send(g)

    partner = row + 1 - 2 * lax.rem(row, 2)

    def ag_copy(g, message, slot, peer):
        block = dall.at[g, part(slot, TOK), :]
        return remote(block, block, ag_s.at[g, message], ag_r.at[g, slot], dp=peer)

    def along_x(i):
        return lax.rem(row + 2 + 2 * i, N_DP)

    def ag_send(g, wait=False):
        each(SIDE - 1, lambda i: go(ag_copy(g, i, row, along_x(i)), wait))
        go(ag_copy(g, SIDE - 1, row, partner), wait)

    def ag_relay(g, wait=False):
        def one(i):
            copy = ag_copy(g, SIDE + i, along_x(i), partner)
            if not wait:
                copy.wait_recv()
            go(copy, wait)

        each(SIDE - 1, one)

    def home(g):
        dk_sum[0] = dk_own[g]
        for rows in (1, 2):
            @pl.when(y + rows < SIDE)
            def _():
                dc_copy(g, rows).wait_recv()
                dk_sum[0] = dk_sum[0] + dk_col[g, rows - 1].astype(F32)

        half = dk_sum[0].astype(BF16)
        dall[g, part(row, TOK), :] = half
        ag_send(g)
        dkvt[part(g, PAIR), :] = half.T

    def rs_copy(g, i, slot, peer):
        return remote(
            w_out.at[g, part(peer, D_OWN), :], w_in.at[g, slot],
            rs_s.at[g, i], rs_r.at[g, slot], seq=peer,
        )

    def rs_send(g, wait=False):
        each(N_SEQ - 1, lambda i: go(rs_copy(g, i, me, other(me, i, N_SEQ)), wait))

    def product(g):
        ag_relay(g)
        each(SIDE, lambda i: ag_copy(g, 0, lax.rem(partner + 2 * i, N_DP), partner).wait_recv())

        w_out[g] = dot(hxt[...], dall[g]).astype(BF16)
        rs_send(g)

    def finish(g):
        def arrive(i, total):
            peer = other(me, i, N_SEQ)
            rs_copy(g, i, peer, peer).wait_recv()
            return total + w_in[g, peer].astype(F32)

        own = w_out[g, part(me, D_OWN), :].astype(F32)
        wgr[:, part(g, PAIR)] = lax.fori_loop(0, N_SEQ - 1, arrive, own) * FACTOR

    def hgr_copy(i):
        cols = part(i, HG)
        return pltpu.make_async_copy(hgr.at[:, cols], hgrad_hbm.at[:, cols], out_sem.at[2, i])

    def hidden_gradient(g, i):
        cols = part(i, HG)
        term = dot(wgt[g, cols, :], dkvt[part(g, PAIR), :])

        @pl.when(g == 0)
        def _():
            hgr_sum[cols, :] = term

        @pl.when((g > 0) & (g < GROUPS - 1))
        def _():
            hgr_sum[cols, :] += term

        @pl.when(g == GROUPS - 1)
        def _():
            hgr[:, cols] = (hgr_sum[cols, :] + term).T.astype(BF16)
            hgr_copy(i).start()

    def stage(g):
        kv_rest(g)

        @pl.when(g == 0)
        def _():
            kv_third(1)

        forward(g)

        @pl.when(g == 0)
        def _():
            kv_second(3)

        @pl.when(g < 2)
        def _():
            kv_third(g + 2)

        @pl.when(g == 2)
        def _():
            hx_arrive()

        @pl.when(g >= 2)
        def _():
            row_sum(g - 2)

        each(KEYS // BLOCK, lambda b: backward(g, b))
        query_gradient(g)


    def hidden_part(g):
        each(D // HG, lambda i: hidden_gradient(g, i))

    each(GROUPS, stage)
    home(0)
    hidden_part(0)
    row_sum(2)
    home(1)
    hidden_part(1)
    product(0)
    row_sum(3)
    home(2)
    product(1)
    hidden_part(2)
    home(3)
    product(2)
    hidden_part(3)
    product(3)
    finish(0)
    finish(1)
    finish(2)

    def drain(g):
        kv_first(g, True)
        kv_row(g, True)
        kv_second(g, True)

        @pl.when(g > 0)
        def _():
            kv_third(g, True)

        each(BACK, lambda i: dk_send(g, i, True))
        dc_send(g, True)
        ag_send(g, True)
        ag_relay(g, True)
        att_copy(g).wait()
        qgr_copy(g).wait()

    each(GROUPS, drain)
    each(N_DP - 1, lambda i: hx_copy(i, row, other(row, i, N_DP)).wait_send())
    each(D // HG, lambda i: hgr_copy(i).wait())
    finish(3)
    wgr_copy = pltpu.make_async_copy(wgr, wgrad_hbm, in_sem.at[4])
    wgr_copy.start()

    def rs_end(g):
        rs_send(g, True)

    each(GROUPS, rs_end)
    wgr_copy.wait()


def settle(a_in, b_in, c_in, d_in, a_out, b_out, c_out, d_out, a, b, c, d, sems):
    parts = []
    for src, mid, dst in ((a_in, a, a_out), (b_in, b, b_out), (c_in, c, c_out), (d_in, d, d_out)):
        half = src.shape[0] // 2
        for h in range(2):
            rows = pl.ds(h * half, half)
            k = len(parts)
            parts.append((
                pltpu.make_async_copy(src.at[rows], mid.at[rows], sems.at[0, k]),
                pltpu.make_async_copy(mid.at[rows], dst.at[rows], sems.at[1, k]),
            ))
    for fetch, _ in parts:
        fetch.start()
    for fetch, store in parts:
        fetch.wait()
        store.start()
    for _, store in parts:
        store.wait()


def local(hidden, queries, kv_weight, value_projection_bias, cotangent, lengths):
    any_spec = pl.BlockSpec(memory_space=pl.ANY)
    vmem = pltpu.VMEM
    dma = pltpu.SemaphoreType.DMA
    width = GROUPS * GROUP_HEADS * HEAD
    results = pl.pallas_call(
        kernel,
        out_shape=(
            jax.ShapeDtypeStruct((TOK, width), BF16),
            jax.ShapeDtypeStruct((TOK, width), BF16),
            jax.ShapeDtypeStruct((TOK, D), BF16),
            jax.ShapeDtypeStruct((D_OWN, GROUPS * PAIR), F32),
        ),
        in_specs=[
            any_spec,
            any_spec,
            any_spec,
            pl.BlockSpec(memory_space=pltpu.VMEM),
            any_spec,
            pl.BlockSpec(memory_space=pltpu.SMEM),
        ],
        out_specs=(any_spec,) * 4,
        scratch_shapes=[
            vmem((TOK, D), BF16),
            vmem((TOK, width), BF16),
            vmem((TOK, width), BF16),
            vmem((GROUPS, D, PAIR), BF16),
            vmem((GROUPS, KEYS, PAIR), BF16),
            vmem((KEYS, TOK), F32),
            vmem((HEAD, KEYS), BF16),
            vmem((HEAD, KEYS), BF16),
            vmem((GROUP_HEADS * HEAD, HEAD), BF16),
            vmem((GROUP_HEADS * HEAD, HEAD), BF16),
            vmem((HEAD, GROUP_HEADS * HEAD), BF16),
            vmem((1, GROUP_HEADS * HEAD), F32),
            vmem((KEYS, GROUP_HEADS * HEAD), BF16),
            vmem((KEYS, GROUP_HEADS * HEAD), BF16),
            vmem((TOK, width), BF16),
            vmem((TOK, width), BF16),
            vmem((TOK, D), BF16),
            vmem((D, TOK), F32),
            vmem((D_OWN, GROUPS * PAIR), F32),
            vmem((GROUPS, KEYS, PAIR), BF16),
            vmem((GROUPS, SIDE - 1, 2, TOK, PAIR), BF16),
            vmem((3, TOK, PAIR), F32),
            vmem((GROUPS, 2, TOK, PAIR), BF16),
            vmem((GROUPS, 2, TOK, PAIR), BF16),
            vmem((GROUPS, TOK, PAIR), F32),
            vmem((GROUPS * PAIR, TOK), BF16),
            vmem((N_DP * TOK, D_PART), BF16),
            vmem((D_PART, N_DP * TOK), BF16),
            vmem((GROUPS, N_DP * TOK, PAIR), BF16),
            vmem((GROUPS, D_PART, PAIR), BF16),
            vmem((GROUPS, N_SEQ, D_OWN, PAIR), BF16),
            dma((5,)),
            dma((GROUPS,)),
            dma((GROUPS, 13)),
            dma((GROUPS, BACK)),
            dma((GROUPS, SIDE - 1, 2)),
            dma((GROUPS, SIDE - 1, 2)),
            dma((GROUPS, 2)),
            dma((GROUPS, 2)),
            dma((N_DP,)),
            dma((N_DP,)),
            dma((GROUPS, N_DP)),
            dma((GROUPS, N_DP)),
            dma((GROUPS, N_SEQ)),
            dma((GROUPS, N_SEQ)),
            dma((3, 16)),
        ],
        compiler_params=pltpu.CompilerParams(
            collective_id=0, has_side_effects=True, vmem_limit_bytes=60 * 1024 * 1024
        ),
        cost_estimate=pl.CostEstimate(
            flops=14_000_000_000, bytes_accessed=26_000_000, transcendentals=5_000_000
        ),
    )(
        hidden,
        queries,
        kv_weight,
        value_projection_bias.reshape(GROUPS, 1, HEAD),
        cotangent,
        lengths,
    )
    return pl.pallas_call(
        settle,
        out_shape=tuple(jax.ShapeDtypeStruct(r.shape, r.dtype) for r in results),
        in_specs=[any_spec] * 4,
        out_specs=(any_spec,) * 4,
        scratch_shapes=[vmem(r.shape, r.dtype) for r in results] + [dma((2, 8))],
    )(*results)


def solution(mesh):
    both = P(("dp", "seq"), None)
    return jax.shard_map(
        local,
        mesh=mesh,
        in_specs=(both, both, P(), P(), both, P("dp", None)),
        out_specs=(both,) * 4,
        check_vma=False,
    )
```

```python
import functools
import math

import jax
import jax.numpy as jnp
from jax import lax
from jax.experimental import pallas as pl
from jax.experimental.pallas import tpu as pltpu
from jax.sharding import PartitionSpec as P

GROUPS = 4
GROUP_HEADS = 8
HEAD = 128
PAIR = 2 * HEAD
TOK = 128
BACK = 8
SLOTS = BACK + 1
KEYS = SLOTS * TOK
D = 8192
N_DP = 8
N_SEQ = 16
D_PART = D // N_DP
D_OWN = D_PART // N_SEQ
SIDE = 4
BLOCK = 3 * TOK
HG = 4096
SCALE = 1.0 / math.sqrt(HEAD)
LOG2E = 1.4426950408889634
FACTOR = 1.0 / math.sqrt(TOK * N_DP * N_SEQ)
F32 = jnp.float32
BF16 = jnp.bfloat16


def dot(a, b):
    return jnp.dot(a, b, preferred_element_type=F32)


def kernel(
    hidden_hbm, queries_hbm, weight_hbm, bias_ref, cot_hbm, lengths_ref,
    att_hbm, qgrad_hbm, hgrad_hbm, wgrad_hbm,
    hid, qry, cot, wgt, kv, mask, kt, vt, q_rows, o_rows, o_cols, delta, prob, dscore, att, qgr, hgr, hgr_sum, wgr,
    dk_out, dk_in, dk_sum, dk_row, dk_col, dk_own, dkvt, hx, hxt, dall,
    w_out, w_in,
    in_sem, wgt_sem, kv_s, kv_r, dk_s, dk_r, dc_s, dc_r, hx_s, hx_r, ag_s, ag_r,
    rs_s, rs_r, out_sem,
):
    me = lax.axis_index("seq")
    row = lax.axis_index("dp")
    y, z = me // SIDE, lax.rem(me, SIDE)

    def remote(src, dst, send, recv, **peer):
        return pltpu.make_async_remote_copy(
            src_ref=src, dst_ref=dst, send_sem=send, recv_sem=recv, device_id=peer,
            device_id_type=pl.DeviceIdType.MESH,
        )

    def part(index, size):
        return pl.ds(pl.multiple_of(index * size, size), size)

    def each(count, body):
        def step(i, _):
            body(i)
            return 0

        lax.fori_loop(0, count, step, 0)

    def other(mine, i, count):
        return lax.rem(mine + 1 + i, count)

    def go(copy, wait):
        if wait:
            copy.wait_send()
        else:
            copy.start()

    in_hid = pltpu.make_async_copy(hidden_hbm, hid, in_sem.at[0])
    in_qry = pltpu.make_async_copy(queries_hbm, qry, in_sem.at[1])
    in_cot = pltpu.make_async_copy(cot_hbm, cot, in_sem.at[2])
    in_hid.start()

    def weight_copy(g):
        return pltpu.make_async_copy(weight_hbm.at[:, part(g, PAIR)], wgt.at[g], wgt_sem.at[g])

    weight_copy(0).start()
    weight_copy(1).start()

    barrier = pltpu.get_barrier_semaphore()

    def greet(**peer):
        pl.semaphore_signal(
            barrier, inc=1, device_id=peer, device_id_type=pl.DeviceIdType.MESH
        )

    each(N_SEQ - 1, lambda i: greet(seq=other(me, i, N_SEQ)))
    each(N_DP - 1, lambda i: greet(dp=other(row, i, N_DP)))

    p_pos = me * TOK + lax.broadcasted_iota(jnp.int32, (1, TOK), 1)
    start = jnp.zeros((1, TOK), jnp.int32)
    end = jnp.int32(0)
    for i in range(lengths_ref.shape[1]):
        end = end + lengths_ref[0, i]
        start = jnp.where(p_pos >= end, end, start)
    k_pos = (me - BACK) * TOK + lax.broadcasted_iota(jnp.int32, (KEYS, TOK), 0)
    mask[...] = jnp.where((k_pos >= start) & (k_pos <= p_pos), 0.0, -1e30).astype(F32)

    def clear(s):
        for g in range(GROUPS):
            kv[g, part(s, TOK), :] = jnp.zeros((TOK, PAIR), BF16)

    each(jnp.maximum(BACK - me, 0), clear)

    in_hid.wait()

    def project(g):
        weight_copy(g).wait()

        @pl.when(g + 2 < GROUPS)
        def _():
            weight_copy(g + 2).start()

        def step(i, total):
            cols = part(i, 4096)
            return total + dot(hid[:, cols], wgt[g, cols, :])

        total = lax.fori_loop(0, D // 4096, step, jnp.zeros((TOK, PAIR), F32))
        kv[g, BACK * TOK :, :HEAD] = total[:, :HEAD].astype(BF16)
        kv[g, BACK * TOK :, HEAD:] = (total[:, HEAD:] + bias_ref[g]).astype(BF16)

    project(0)
    pl.semaphore_wait(barrier, N_SEQ - 1 + N_DP - 1)

    def kv_send(g, message, src, dst, peer):
        return remote(
            kv.at[g, part(src, TOK), :], kv.at[g, part(dst, TOK), :],
            kv_s.at[g, message], kv_r.at[g, dst], seq=peer,
        )

    def along_z(g, i, first, slot, wait):
        to = other(z, i, SIDE)
        dst = jnp.clip(slot + z - to, 0, BACK - 1)
        go(kv_send(g, first + i, slot, dst, y * SIDE + to), wait)

    def kv_first(g, wait=False):
        for rows in (1, 2):
            @pl.when(y + rows < SIDE)
            def _():
                to = jnp.minimum(me + SIDE * rows, N_SEQ - 1)
                go(kv_send(g, rows - 1, BACK, BACK - SIDE * rows, to), wait)

    def sent(g, i):
        return (i != 1) | (g == 0)

    def kv_row(g, wait=False):
        def own(i):
            @pl.when((other(z, i, SIDE) > z) & sent(g, i))
            def _():
                along_z(g, i, 2, BACK, wait)

        each(SIDE - 1, own)

    def kv_arrive(g, s):
        kv_send(g, 0, BACK, s, me).wait_recv()

    def kv_second(g, wait=False):
        if not wait:
            @pl.when(g > 0)
            def _():
                kv_row(g)

        @pl.when(y >= 1)
        def _():
            if not wait:
                kv_arrive(g, SIDE)

            def row_before(i):
                @pl.when(sent(g, i))
                def _():
                    along_z(g, i, 5, SIDE, wait)

            each(SIDE - 1, row_before)

        @pl.when(y >= 2)
        def _():
            if not wait:
                kv_arrive(g, 0)

            def two_before(i):
                @pl.when((other(z, i, SIDE) < z) & sent(g, i))
                def _():
                    along_z(g, i, 8, 0, wait)

            each(SIDE - 1, two_before)

    up_from = jnp.where(z == SIDE - 1, 3, 7)
    down_from = jnp.where(z == 0, 5, 1)

    def kv_third(g, wait=False):
        for message, src, dst, to in (
            (11, up_from, 6, y * SIDE + lax.rem(z + 1, SIDE)),
            (12, down_from, 2, y * SIDE + lax.rem(z + SIDE - 1, SIDE)),
        ):
            @pl.when(me + src >= BACK)
            def _():
                if not wait:
                    kv_arrive(g, src)
                go(kv_send(g, message, src, dst, to), wait)

    def kv_rest(g):
        def arrive(s):
            passed = (g > 0) & ((s == up_from) | (s == down_from))

            @pl.when((lax.rem(s, SIDE) != 0) & (me + s >= BACK) & jnp.logical_not(passed))
            def _():
                kv_arrive(g, s)

        each(BACK, arrive)

    def hx_copy(i, slot, peer):
        return remote(
            hid.at[:, part(peer, D_PART)], hx.at[part(slot, TOK), :],
            hx_s.at[i], hx_r.at[slot], dp=peer,
        )

    hx_own = pltpu.make_async_copy(
        hid.at[:, part(row, D_PART)], hx.at[part(row, TOK), :], in_sem.at[3]
    )
    def prepare(t):
        @pl.when(t > 0)
        def _():
            project(t)

        kv_first(t)

        @pl.when(t == 0)
        def _():
            kv_row(t)

        @pl.when(t == 0)
        def _():
            each(N_DP - 1, lambda i: hx_copy(i, row, other(row, i, N_DP)).start())
            hx_own.start()
            in_qry.start()
            in_cot.start()

        @pl.when(t >= 2)
        def _():
            kv_second(t - 2)

    each(GROUPS, prepare)
    kv_second(2)
    in_qry.wait()
    in_cot.wait()

    def hx_arrive():
        def arrive(i):
            peer = other(row, i, N_DP)
            hx_copy(i, peer, peer).wait_recv()

        each(N_DP - 1, arrive)
        hx_own.wait()

        hxt[...] = hx[...].T

    def att_copy(g):
        cols = part(g, 1024)
        return pltpu.make_async_copy(att.at[:, cols], att_hbm.at[:, cols], out_sem.at[0, g])

    def qgr_copy(g):
        cols = part(g, 1024)
        return pltpu.make_async_copy(qgr.at[:, cols], qgrad_hbm.at[:, cols], out_sem.at[1, g])

    WIDE = GROUP_HEADS * HEAD

    def stacked(wide):
        return jnp.concatenate([wide[:, h * HEAD : (h + 1) * HEAD] for h in range(GROUP_HEADS)], 0)

    def turned(wide):
        return jnp.concatenate([wide[:, h * HEAD : (h + 1) * HEAD].T for h in range(GROUP_HEADS)], 1)

    def forward(g):
        kt[...] = kv[g, :, :HEAD].T
        vt[...] = kv[g, :, HEAD:].T
        cols = part(g, WIDE)
        q_wide = qry[:, cols]
        o_wide = cot[:, cols]
        q_rows[...] = stacked(q_wide)
        o_rows[...] = stacked(o_wide)
        turned_o = turned(o_wide)
        o_cols[...] = turned_o
        s = dot(kv[g, :, :HEAD], turned(q_wide)) + jnp.concatenate([mask[...]] * GROUP_HEADS, 1)
        top = jnp.max(s, axis=0, keepdims=True)
        e = jnp.exp2((s - top) * (SCALE * LOG2E))
        inv = 1.0 / jnp.sum(e, axis=0, keepdims=True)
        half = (e * inv).astype(BF16)
        prob[...] = half
        out = dot(vt[...], half)
        out_b = out.astype(BF16).astype(F32)
        delta[...] = jnp.sum(turned_o.astype(F32) * out_b, axis=0, keepdims=True)
        att[:, cols] = turned(out).astype(BF16)
        att_copy(g).start()

    def backward(g, b):
        rows = part(b, BLOCK)
        half = prob[rows, :]
        dp = dot(kv[g, rows, HEAD:], o_cols[...])
        ds = (half.astype(F32) * (dp - delta[...])).astype(BF16)
        dscore[rows, :] = ds
        dk = dot(ds, q_rows[...]) * SCALE
        dv = dot(half, o_rows[...])
        dk_out[g, rows, :HEAD] = dk.astype(BF16)
        dk_out[g, rows, HEAD:] = dv.astype(BF16)
        dk_own[g, :, :HEAD] = dk[BLOCK - TOK :]
        dk_own[g, :, HEAD:] = dv[BLOCK - TOK :]
        each(BLOCK // TOK, lambda i: dk_send(g, b * (BLOCK // TOK) + i))

    def query_gradient(g):
        qgr[:, part(g, WIDE)] = turned(dot(kt[...], dscore[...]) * SCALE).astype(BF16)
        qgr_copy(g).start()

    def dk_copy(g, w, a, to):
        return remote(
            dk_out.at[g, part(w + SIDE * a, TOK), :], dk_in.at[g, w - 1, a],
            dk_s.at[g, w - 1, a], dk_r.at[g, w - 1, a], seq=to,
        )

    def dk_send(g, slot, wait=False):
        w, a = lax.rem(slot, SIDE), slot // SIDE

        @pl.when((w != 0) & (slot < BACK) & (me + slot >= BACK))
        def _():
            go(dk_copy(g, jnp.maximum(w, 1), a, y * SIDE + lax.rem(z + w, SIDE)), wait)

    def dc_copy(g, rows):
        return remote(
            dk_row.at[g, rows - 1], dk_col.at[g, rows - 1],
            dc_s.at[g, rows - 1], dc_r.at[g, rows - 1],
            seq=jnp.maximum(me - SIDE * rows, 0),
        )

    def dc_send(g, wait=False):
        for rows in (1, 2):
            @pl.when(y >= rows)
            def _():
                go(dc_copy(g, rows), wait)

    def row_sum(g):
        dk_sum[0] = dk_own[g]
        dk_sum[1] = dk_out[g, SIDE * TOK : (SIDE + 1) * TOK, :].astype(F32)
        dk_sum[2] = dk_out[g, :TOK, :].astype(F32)
        for w in range(1, SIDE):
            source = y * SIDE + lax.rem(z + SIDE - w, SIDE)
            nearer = jnp.where(z < w, 0, 1)
            for a in range(2):
                @pl.when(source + w + SIDE * a >= BACK)
                def _():
                    dk_copy(g, w, a, me).wait_recv()
                    at = nearer + 1 - a
                    dk_sum[at] = dk_sum[at] + dk_in[g, w - 1, a].astype(F32)

        dk_own[g] = dk_sum[0]
        dk_row[g, 0] = dk_sum[1].astype(BF16)
        dk_row[g, 1] = dk_sum[2].astype(BF16)
        dc_send(g)

    partner = row + 1 - 2 * lax.rem(row, 2)

    def ag_copy(g, message, slot, peer):
        block = dall.at[g, part(slot, TOK), :]
        return remote(block, block, ag_s.at[g, message], ag_r.at[g, slot], dp=peer)

    def along_x(i):
        return lax.rem(row + 2 + 2 * i, N_DP)

    def ag_send(g, wait=False):
        each(SIDE - 1, lambda i: go(ag_copy(g, i, row, along_x(i)), wait))
        go(ag_copy(g, SIDE - 1, row, partner), wait)

    def ag_relay(g, wait=False):
        def one(i):
            copy = ag_copy(g, SIDE + i, along_x(i), partner)
            if not wait:
                copy.wait_recv()
            go(copy, wait)

        each(SIDE - 1, one)

    def home(g):
        dk_sum[0] = dk_own[g]
        for rows in (1, 2):
            @pl.when(y + rows < SIDE)
            def _():
                dc_copy(g, rows).wait_recv()
                dk_sum[0] = dk_sum[0] + dk_col[g, rows - 1].astype(F32)

        half = dk_sum[0].astype(BF16)
        dall[g, part(row, TOK), :] = half
        ag_send(g)
        dkvt[part(g, PAIR), :] = half.T

    def rs_copy(g, i, slot, peer):
        return remote(
            w_out.at[g, part(peer, D_OWN), :], w_in.at[g, slot],
            rs_s.at[g, i], rs_r.at[g, slot], seq=peer,
        )

    def rs_send(g, wait=False):
        each(N_SEQ - 1, lambda i: go(rs_copy(g, i, me, other(me, i, N_SEQ)), wait))

    def product(g):
        ag_relay(g)
        each(SIDE, lambda i: ag_copy(g, 0, lax.rem(partner + 2 * i, N_DP), partner).wait_recv())

        w_out[g] = dot(hxt[...], dall[g]).astype(BF16)
        rs_send(g)

    def finish(g):
        def arrive(i, total):
            peer = other(me, i, N_SEQ)
            rs_copy(g, i, peer, peer).wait_recv()
            return total + w_in[g, peer].astype(F32)

        own = w_out[g, part(me, D_OWN), :].astype(F32)
        wgr[:, part(g, PAIR)] = lax.fori_loop(0, N_SEQ - 1, arrive, own) * FACTOR

    def hgr_copy(i):
        cols = part(i, HG)
        return pltpu.make_async_copy(hgr.at[:, cols], hgrad_hbm.at[:, cols], out_sem.at[2, i])

    def hidden_gradient(g, i):
        cols = part(i, HG)
        term = dot(wgt[g, cols, :], dkvt[part(g, PAIR), :])

        @pl.when(g == 0)
        def _():
            hgr_sum[cols, :] = term

        @pl.when((g > 0) & (g < GROUPS - 1))
        def _():
            hgr_sum[cols, :] += term

        @pl.when(g == GROUPS - 1)
        def _():
            hgr[:, cols] = (hgr_sum[cols, :] + term).T.astype(BF16)
            hgr_copy(i).start()

    def stage(g):
        kv_rest(g)

        @pl.when(g == 0)
        def _():
            kv_third(1)

        forward(g)

        @pl.when(g == 0)
        def _():
            kv_second(3)

        @pl.when(g < 2)
        def _():
            kv_third(g + 2)

        @pl.when(g == 2)
        def _():
            hx_arrive()

        @pl.when(g >= 2)
        def _():
            row_sum(g - 2)

        @pl.when(g == 3)
        def _():
            home(0)

        each(KEYS // BLOCK, lambda b: backward(g, b))
        query_gradient(g)


    def hidden_part(g):
        each(D // HG, lambda i: hidden_gradient(g, i))

    each(GROUPS, stage)
    hidden_part(0)
    row_sum(2)
    home(1)
    hidden_part(1)
    row_sum(3)
    product(0)
    home(2)
    product(1)
    hidden_part(2)
    home(3)
    product(2)
    hidden_part(3)
    product(3)
    finish(0)
    finish(1)
    finish(2)

    def drain(g):
        kv_first(g, True)
        kv_row(g, True)
        kv_second(g, True)

        @pl.when(g > 0)
        def _():
            kv_third(g, True)

        each(BACK, lambda i: dk_send(g, i, True))
        dc_send(g, True)
        ag_send(g, True)
        ag_relay(g, True)
        att_copy(g).wait()
        qgr_copy(g).wait()

    each(GROUPS, drain)
    each(N_DP - 1, lambda i: hx_copy(i, row, other(row, i, N_DP)).wait_send())
    each(D // HG, lambda i: hgr_copy(i).wait())
    finish(3)
    wgr_copy = pltpu.make_async_copy(wgr, wgrad_hbm, in_sem.at[4])
    wgr_copy.start()

    def rs_end(g):
        rs_send(g, True)

    each(GROUPS, rs_end)
    wgr_copy.wait()


def settle(a_in, b_in, c_in, d_in, a_out, b_out, c_out, d_out, a, b, c, d, sems):
    parts = []
    for src, mid, dst in ((a_in, a, a_out), (b_in, b, b_out), (c_in, c, c_out), (d_in, d, d_out)):
        half = src.shape[0] // 2
        for h in range(2):
            rows = pl.ds(h * half, half)
            k = len(parts)
            parts.append((
                pltpu.make_async_copy(src.at[rows], mid.at[rows], sems.at[0, k]),
                pltpu.make_async_copy(mid.at[rows], dst.at[rows], sems.at[1, k]),
            ))
    for fetch, _ in parts:
        fetch.start()
    for fetch, store in parts:
        fetch.wait()
        store.start()
    for _, store in parts:
        store.wait()


def local(hidden, queries, kv_weight, value_projection_bias, cotangent, lengths):
    any_spec = pl.BlockSpec(memory_space=pl.ANY)
    vmem = pltpu.VMEM
    dma = pltpu.SemaphoreType.DMA
    width = GROUPS * GROUP_HEADS * HEAD
    results = pl.pallas_call(
        kernel,
        out_shape=(
            jax.ShapeDtypeStruct((TOK, width), BF16),
            jax.ShapeDtypeStruct((TOK, width), BF16),
            jax.ShapeDtypeStruct((TOK, D), BF16),
            jax.ShapeDtypeStruct((D_OWN, GROUPS * PAIR), F32),
        ),
        in_specs=[
            any_spec,
            any_spec,
            any_spec,
            pl.BlockSpec(memory_space=pltpu.VMEM),
            any_spec,
            pl.BlockSpec(memory_space=pltpu.SMEM),
        ],
        out_specs=(any_spec,) * 4,
        scratch_shapes=[
            vmem((TOK, D), BF16),
            vmem((TOK, width), BF16),
            vmem((TOK, width), BF16),
            vmem((GROUPS, D, PAIR), BF16),
            vmem((GROUPS, KEYS, PAIR), BF16),
            vmem((KEYS, TOK), F32),
            vmem((HEAD, KEYS), BF16),
            vmem((HEAD, KEYS), BF16),
            vmem((GROUP_HEADS * HEAD, HEAD), BF16),
            vmem((GROUP_HEADS * HEAD, HEAD), BF16),
            vmem((HEAD, GROUP_HEADS * HEAD), BF16),
            vmem((1, GROUP_HEADS * HEAD), F32),
            vmem((KEYS, GROUP_HEADS * HEAD), BF16),
            vmem((KEYS, GROUP_HEADS * HEAD), BF16),
            vmem((TOK, width), BF16),
            vmem((TOK, width), BF16),
            vmem((TOK, D), BF16),
            vmem((D, TOK), F32),
            vmem((D_OWN, GROUPS * PAIR), F32),
            vmem((GROUPS, KEYS, PAIR), BF16),
            vmem((GROUPS, SIDE - 1, 2, TOK, PAIR), BF16),
            vmem((3, TOK, PAIR), F32),
            vmem((GROUPS, 2, TOK, PAIR), BF16),
            vmem((GROUPS, 2, TOK, PAIR), BF16),
            vmem((GROUPS, TOK, PAIR), F32),
            vmem((GROUPS * PAIR, TOK), BF16),
            vmem((N_DP * TOK, D_PART), BF16),
            vmem((D_PART, N_DP * TOK), BF16),
            vmem((GROUPS, N_DP * TOK, PAIR), BF16),
            vmem((GROUPS, D_PART, PAIR), BF16),
            vmem((GROUPS, N_SEQ, D_OWN, PAIR), BF16),
            dma((5,)),
            dma((GROUPS,)),
            dma((GROUPS, 13)),
            dma((GROUPS, BACK)),
            dma((GROUPS, SIDE - 1, 2)),
            dma((GROUPS, SIDE - 1, 2)),
            dma((GROUPS, 2)),
            dma((GROUPS, 2)),
            dma((N_DP,)),
            dma((N_DP,)),
            dma((GROUPS, N_DP)),
            dma((GROUPS, N_DP)),
            dma((GROUPS, N_SEQ)),
            dma((GROUPS, N_SEQ)),
            dma((3, 16)),
        ],
        compiler_params=pltpu.CompilerParams(
            collective_id=0, has_side_effects=True, vmem_limit_bytes=60 * 1024 * 1024
        ),
        cost_estimate=pl.CostEstimate(
            flops=14_000_000_000, bytes_accessed=26_000_000, transcendentals=5_000_000
        ),
    )(
        hidden,
        queries,
        kv_weight,
        value_projection_bias.reshape(GROUPS, 1, HEAD),
        cotangent,
        lengths,
    )
    return pl.pallas_call(
        settle,
        out_shape=tuple(jax.ShapeDtypeStruct(r.shape, r.dtype) for r in results),
        in_specs=[any_spec] * 4,
        out_specs=(any_spec,) * 4,
        scratch_shapes=[vmem(r.shape, r.dtype) for r in results] + [dma((2, 8))],
    )(*results)


def solution(mesh):
    both = P(("dp", "seq"), None)
    return jax.shard_map(
        local,
        mesh=mesh,
        in_specs=(both, both, P(), P(), both, P("dp", None)),
        out_specs=(both,) * 4,
        check_vma=False,
    )
```
